256 devices in a mesh: video: 4 (over z_lo), slab: 64 (over y, x, z_hi, core).
Axes of the slice: x: 4, y: 4, z: 8 (z_hi: 2, z_lo: 4; z = z_hi * 4 + z_lo), core: 2. Of those that a mesh axis runs over, the one named last changes fastest.
Arguments:
- section_input: bfloat16 [24, 96, 256, 128], P('video', None, 'slab'), parts along dimension 0, may hold values from -6 to 6
- main_cache: bfloat16 [8, 96, 256, 128], P('video', None, 'slab'), parts along dimension 0, may hold values from -5 to 5
- head_cache: bfloat16 [8, 96, 256, 128], P('video', None, 'slab'), parts along dimension 0, may hold values from -5 to 5
- gain_in: float32 [96], replicated, may hold values from 0.25 to 1.75
- gain_out: float32 [96], replicated, may hold values from 0.25 to 1.75
- main_weight: bfloat16 [3, 3, 3, 96, 96], replicated, may hold values from -0.125 to 0.125
- head_weight: bfloat16 [3, 3, 3, 3, 96], replicated, may hold values from -0.125 to 0.125
- aspect_grad: bfloat16 [24, 4, 256, 128], P('video', None, 'slab'), parts along dimension 0, may hold values from -6 to 6
- aspect_table: float32 [16, 3, 4], replicated, may hold values from -4 to 4
- aspect_index: int32 [24], P('video'), parts along dimension 0, may hold values from 0 to 15
- frame_order: int32 [6], replicated, may hold values from 0 to 5, each once
Outputs:
- grad_input: float32 [24, 96, 256, 128], P('video', None, 'slab'), parts along dimension 0
- grad_main_weight: float32 [12, 3, 3, 96, 96], P('video'), parts along dimension 0
- grad_head_weight: float32 [12, 3, 3, 3, 96], P('video'), parts along dimension 0
The draws below stay inside these ranges and needn't reach their ends.
There are 4 independent parts, one for each index of `video`. The reference program is written for one: setup_inputs(seed, part) draws one part's arguments, and reference() takes and returns one part's arrays. A program takes and returns all parts, laid end to end along the dimension named above; an argument that names none is the same for every part. Nothing has to cross between parts.
All inputs are finite; a program needn't handle non-finite values.
Results may differ from the reference program's by a relative error of at most 0.015.
Values may be sent and summed in bfloat16 or wider, within the bound.
A program may use at most 128 MiB of HBM per device.

```python
import jax
import jax.numpy as jnp
from jax import lax

C = 96
FR = 6
CTX = 2
W = 128
ASP = 4
NASP = 16
H = 256


def set_ends(array, own_key, smallest, largest):
    index_at = [jax.random.randint(jax.random.fold_in(own_key, axis), (), 0, length) for axis, length in enumerate(array.shape)]
    main_axis = array.shape.index(max(array.shape))
    next_to = index_at[:main_axis] + [(index_at[main_axis] + 1) % array.shape[main_axis]] + index_at[main_axis + 1:]
    return array.at[tuple(index_at)].set(smallest).at[tuple(next_to)].set(largest)


def level_of(rng, dims, split, smallest, top_value):
    level = 1.0
    for axis_at, parts in split:
        steps = jax.random.uniform(jax.random.fold_in(jax.random.fold_in(rng, 6), axis_at), (parts,), jnp.float32, smallest / len(split), top_value / len(split))
        level = level * jnp.repeat(jnp.exp(steps), dims[axis_at] // parts).reshape((-1,) + (1,) * (len(dims) - 1 - axis_at))
    return level


def noise(stream_key, dims, deviation, limit, pieces=(), held_as=jnp.bfloat16):
    drawn = deviation * jax.random.normal(stream_key, dims, jnp.float32)
    if pieces:
        drawn = drawn * level_of(stream_key, dims, pieces, -0.22, 0.18)
    return jnp.clip(drawn, -limit, limit).astype(held_as)


def setup_inputs(seed: int = 0, part: int = 0) -> dict:
    streams_of = jax.random.split(jax.random.key(seed), 12)
    part_keys = jax.random.split(jax.random.fold_in(streams_of[11], part), 12)
    section_input = noise(part_keys[0], (FR, C, H, W), 1.0, 6.0, ((2, 64),))
    main_cache = noise(part_keys[1], (CTX, C, H, W), 0.7, 5.0, ((2, 64),))
    head_cache = noise(part_keys[2], (CTX, C, H, W), 0.7, 5.0, ((2, 64),))
    gain_in = jnp.clip(1.0 + 0.15 * jax.random.normal(streams_of[3], (C,), jnp.float32), 0.25, 1.75)
    gain_out = jnp.clip(1.0 + 0.15 * jax.random.normal(streams_of[4], (C,), jnp.float32), 0.25, 1.75)
    main_weight = noise(streams_of[5], (3, 3, 3, C, C), (27 * C) ** -0.5, 0.125)
    head_weight = noise(streams_of[6], (3, 3, 3, 3, C), (27 * C) ** -0.5, 0.125)
    aspect_grad = noise(part_keys[7], (FR, ASP, H, W), 1.0, 6.0, ((2, 64),))
    aspect_table = noise(streams_of[8], (NASP, 3, ASP), 1.0, 4.0, (), jnp.float32)
    aspect_index = set_ends(jax.random.randint(part_keys[9], (FR,), 0, NASP), jax.random.fold_in(part_keys[9], 1), 0, NASP - 1).astype(jnp.int32)
    frame_order = jax.random.permutation(streams_of[10], FR).astype(jnp.int32)
    return {"section_input": section_input, "main_cache": main_cache, "head_cache": head_cache, "gain_in": gain_in, "gain_out": gain_out, "main_weight": main_weight, "head_weight": head_weight, "aspect_grad": aspect_grad, "aspect_table": aspect_table, "aspect_index": aspect_index, "frame_order": frame_order}


EPS = 1e-06

def norm_silu(value, gain):
    meansq = lax.optimization_barrier(jnp.mean(value * value, axis=1, keepdims=True))
    normed = value * lax.rsqrt(meansq + EPS) * gain[None, :, None, None]
    return normed * jax.nn.sigmoid(normed)

def conv_forward(hin, weight):
    frames = hin.shape[0] - 2
    rows = hin.shape[2]
    cols = hin.shape[3]
    padded = jnp.pad(hin.astype(jnp.float32), ((0, 0), (0, 0), (1, 1), (1, 1)))
    wfloat = weight.astype(jnp.float32)
    total = jnp.zeros((frames, weight.shape[3], rows, cols), jnp.float32)
    for t in range(3):
        for y in range(3):
            for x in range(3):
                total = total + jnp.einsum('oc,fchw->fohw', wfloat[t, y, x], padded[t:t + frames, :, y:y + rows, x:x + cols])
    return total

def conv_transpose(grad, weight):
    frames = grad.shape[0]
    rows = grad.shape[2]
    cols = grad.shape[3]
    padded = jnp.pad(grad.astype(jnp.float32), ((0, 0), (0, 0), (1, 1), (1, 1)))
    wfloat = weight.astype(jnp.float32)
    full = jnp.zeros((frames + 2, weight.shape[4], rows, cols), jnp.float32)
    for t in range(3):
        for y in range(3):
            for x in range(3):
                term = jnp.einsum('oc,fohw->fchw', wfloat[t, y, x], padded[:, :, 2 - y:2 - y + rows, 2 - x:2 - x + cols])
                full = full.at[t:t + frames].add(term)
    return full[2:]

def weight_grad(grad, hin):
    frames = grad.shape[0]
    rows = grad.shape[2]
    cols = grad.shape[3]
    padded = jnp.pad(hin.astype(jnp.float32), ((0, 0), (0, 0), (1, 1), (1, 1)))
    gfloat = grad.astype(jnp.float32)
    result = []
    for t in range(3):
        for y in range(3):
            for x in range(3):
                result.append(jnp.einsum('fohw,fchw->oc', gfloat, padded[t:t + frames, :, y:y + rows, x:x + cols]))
    stacked = jnp.stack(result, 0)
    return stacked.reshape((3, 3, 3) + stacked.shape[1:])

def reference(section_input, main_cache, head_cache, gain_in, gain_out, main_weight, head_weight, aspect_grad, aspect_table, aspect_index, frame_order):
    xfloat = section_input.astype(jnp.float32)
    hidden = norm_silu(xfloat, gain_in).astype(jnp.bfloat16)
    hin = jnp.concatenate([main_cache, hidden], 0)
    out = xfloat + conv_forward(hin, main_weight)
    head_hidden = norm_silu(out, gain_out).astype(jnp.bfloat16)
    headin = jnp.concatenate([head_cache, head_hidden], 0)
    frames = section_input.shape[0]
    owner = (frame_order[None, :] == jnp.arange(frames, dtype=jnp.int32)[:, None]).astype(jnp.float32)
    picked = (aspect_index[:, None] == jnp.arange(aspect_table.shape[0], dtype=jnp.int32)[None, :]).astype(jnp.float32)
    coeff = jnp.einsum('fn,nca->fca', picked, aspect_table.astype(jnp.float32))
    pixel_grad = jnp.einsum('fj,fca,jahw->fchw', owner, coeff, aspect_grad.astype(jnp.float32)).astype(jnp.bfloat16)
    d_hh = conv_transpose(pixel_grad, head_weight)
    head_sum = weight_grad(pixel_grad, headin)
    _, pull_out = jax.vjp(lambda value: norm_silu(value, gain_out), out)
    d_out = pull_out(d_hh)[0]
    d_out_b = d_out.astype(jnp.bfloat16)
    d_hidden = conv_transpose(d_out_b, main_weight)
    main_sum = weight_grad(d_out_b, hin)
    _, pull_in = jax.vjp(lambda value: norm_silu(value, gain_in), xfloat)
    grad_input = d_out + pull_in(d_hidden)[0]
    scale = 1.0 / jnp.sqrt(jnp.float32(frames * section_input.shape[2] * section_input.shape[3]))
    return (grad_input, main_sum * scale, head_sum * scale)
```

```python
import functools

import jax
import jax.numpy as jnp
from jax import lax
from jax.experimental import pallas as pl
from jax.experimental.pallas import tpu as pltpu
from jax.sharding import PartitionSpec as P

EPS = 1e-06
MESH = pl.DeviceIdType.MESH
F32 = jnp.float32
BF16 = jnp.bfloat16
C = 96
FR = 6
COLS = 128
K3 = 9 * C
TILES = 128


def dot(a, b):
    return lax.dot_general(a, b, (((1,), (0,)), ((), ())), preferred_element_type=F32)


def dot_nt(a, b):
    return lax.dot_general(a, b, (((1,), (1,)), ((), ())), preferred_element_type=F32)


def lane_of(value):
    return lax.broadcasted_iota(jnp.int32, value.shape, 1)


def later(value):
    return jnp.where(lane_of(value) == 0, 0.0, pltpu.roll(value, 1, 1))


def earlier(value):
    return jnp.where(lane_of(value) == COLS - 1, 0.0, pltpu.roll(value, COLS - 1, 1))


def by_row(shift, value):
    parts = [shift(value[:, i : i + COLS]) for i in range(0, value.shape[1], COLS)]
    return jnp.concatenate(parts, axis=1)


def wide(gain, width):
    return jnp.concatenate([gain] * (width // COLS), axis=1)


def norm_parts(value, gain):
    meansq = jnp.sum(value * value, axis=0, keepdims=True) * (1.0 / C)
    root = lax.rsqrt(meansq + EPS)
    unit = value * root
    normed = unit * gain
    sig = 0.5 * jnp.tanh(0.5 * normed) + 0.5
    return root, unit, normed, sig


def norm_pull(parts, gain, cot):
    root, unit, normed, sig = parts
    inner = cot * gain * (sig * (1.0 + normed * (1.0 - sig)))
    mean = jnp.sum(inner * unit, axis=0, keepdims=True) * (1.0 / C)
    return root * (inner - unit * mean)


def kernel(
    slabs,
    x_ref,
    mc_ref,
    hc_ref,
    gin_ref,
    gout_ref,
    mw_ref,
    hw_ref,
    ag_ref,
    tab_ref,
    idx_ref,
    ord_ref,
    gi_ref,
    gm_ref,
    gh_ref,
    stage,
    xs,
    gains,
    hin,
    hin_t,
    hin_b,
    head,
    wtmp,
    wf,
    wt,
    hwt,
    pg_own,
    pg_send,
    pg_halo,
    taps,
    dout,
    dob,
    dob_t,
    dob_b,
    dsh,
    grads,
    piece,
    got1,
    sum1,
    got2,
    half3,
    got3,
    full,
    hs,
    hr,
    ps,
    pr,
    ds,
    dr,
    s1,
    r1,
    s2,
    r2,
    s3,
    r3,
    s4,
    r4,
    s5,
    r5,
):
    planes = slabs // 4
    me = lax.axis_index("slab")
    core = me % 2
    place = me % 4
    zh = place // 2
    xy = me // 4
    up = (me + slabs - 1) % slabs
    down = (me + 1) % slabs
    sibling = me + 1 - 2 * core
    zpartner = me + 2 - 4 * zh

    def in_plane(k):
        return ((xy + k) % planes) * 4 + place

    def remote(src, dst, send, recv, to):
        return pltpu.make_async_remote_copy(
            src_ref=src,
            dst_ref=dst,
            send_sem=send,
            recv_sem=recv,
            device_id={"slab": to},
            device_id_type=MESH,
        )

    barrier = pltpu.get_barrier_semaphore()

    def greet(to):
        pl.semaphore_signal(barrier, inc=1, device_id={"slab": to}, device_id_type=MESH)

    greet(up)
    greet(down)
    greet(zpartner)
    for k in range(1, planes):
        greet(in_plane(k))

    def split_rows(f, source):
        stage[f] = source.astype(F32)
        return jnp.concatenate(
            [stage[f, pl.ds(r, C, stride=4), :] for r in range(4)], axis=1
        )

    for j in range(2):
        hin[j] = split_rows(j, mc_ref[j]).astype(BF16)
        head[j] = split_rows(j, hc_ref[j]).astype(BF16)

    pg_own[...] = jnp.zeros_like(pg_own)
    for f in range(FR):
        picked = []
        for a in range(4):
            total = None
            for j in range(FR):
                weight = jnp.where(ord_ref[j] == f, 1.0, 0.0).astype(F32)
                term = ag_ref[j, a].astype(F32) * weight
                total = term if total is None else total + term
            picked.append(total)
        row = idx_ref[f]
        for c in range(3):
            value = picked[0] * tab_ref[row, c, 0]
            for a in range(1, 4):
                value = value + picked[a] * tab_ref[row, c, a]
            for r in range(4):
                pg_own[r, 6 + 3 * f + c : 7 + 3 * f + c, :] = value[r : r + 1, :]
    pg_send[...] = pg_own[...].astype(BF16)

    pl.semaphore_wait(barrier, planes + 2)

    def pg_copy(side):
        return remote(
            pg_send.at[0 if side == 0 else 3],
            pg_halo.at[1 - side],
            ps.at[side],
            pr.at[1 - side],
            up if side == 0 else down,
        )

    for side in range(2):
        pg_copy(side).start()

    def hin_copy(side, f):
        if side == 0:
            return remote(hin.at[f, :, pl.ds(0, COLS)], hin_b.at[f], hs.at[0, f], hr.at[1, f], up)
        return remote(hin.at[f, :, pl.ds(3 * COLS, COLS)], hin_t.at[f], hs.at[1, f], hr.at[0, f], down)

    def dob_copy(side, f):
        if side == 0:
            return remote(dob.at[f, :, pl.ds(0, COLS)], dob_b.at[f], ds.at[0, f], dr.at[1, f], up)
        return remote(dob.at[f, :, pl.ds(3 * COLS, COLS)], dob_t.at[f], ds.at[1, f], dr.at[0, f], down)

    for j in range(2):
        for side in range(2):
            hin_copy(side, j).start()

    gains[0] = jnp.broadcast_to(gin_ref[...], (COLS, C)).T
    gains[1] = jnp.broadcast_to(gout_ref[...], (COLS, C)).T

    def make_h(f, carry):
        value = split_rows(f, x_ref[f])
        xs[f] = value
        _, _, normed, sig = norm_parts(value, wide(gains[0], 4 * COLS))
        hin[f + 2] = (normed * sig).astype(BF16)
        for side in range(2):
            hin_copy(side, f + 2).start()
        return carry

    lax.fori_loop(0, FR, make_h, 0)

    for x in range(3):
        for y in range(3):
            for t in range(3):
                at = (y * 3 + t) * C
                wtmp[0, x * C : (x + 1) * C, at : at + C] = mw_ref[t, y, x].astype(F32)
                wtmp[1, x * C : (x + 1) * C, at : at + C] = mw_ref[2 - t, 2 - y, x].astype(F32).T
    wf[...] = wtmp[0, :, 0:K3].astype(BF16)
    wt[...] = wtmp[1, :, 0:K3].astype(BF16)
    grads[0:C, 0:C] = jnp.zeros((C, C), F32)
    for y in range(3):
        for x in range(3):
            for t in range(3):
                at = y * 32 + x * 9 + t * 3
                grads[at : at + 3, 0:C] = hw_ref[2 - t, y, x].astype(F32)
    hwt[...] = grads[0:C, 0:C].T.astype(BF16)

    for side in range(2):
        pg_copy(side).wait_recv()

    @pl.when(me == 0)
    def _():
        pg_halo[0] = jnp.zeros((32, COLS), BF16)

    @pl.when(me == slabs - 1)
    def _():
        pg_halo[1] = jnp.zeros((32, COLS), BF16)

    rows6 = [pg_halo[0]] + [pg_send[r] for r in range(4)] + [pg_halo[1]]
    rows6 = [value.astype(F32) for value in rows6]
    stack = jnp.concatenate(
        [
            jnp.concatenate([earlier(value) for value in rows6], axis=1),
            jnp.concatenate(rows6, axis=1),
            jnp.concatenate([later(value) for value in rows6], axis=1),
        ],
        axis=0,
    ).astype(BF16)
    out_row = lax.broadcasted_iota(jnp.int32, (8 * 32, C), 0)
    in_row = lax.broadcasted_iota(jnp.int32, (8 * 32, C), 1)
    frame = lax.shift_right_logical(out_row, 5)
    tap = out_row - 32 * frame
    col = jnp.where(tap >= 9, 1, 0) + jnp.where(tap >= 18, 1, 0)
    source = col * 32 + frame * 3 + (tap - 9 * col)
    chosen = jnp.where((in_row == source) & (tap < 27), 1.0, 0.0).astype(BF16)
    spread = dot(chosen, stack).astype(BF16)
    for f in range(8):
        taps[f] = spread[f * 32 : (f + 1) * 32, :]

    def pixel_taps(f, first, rows):
        return jnp.concatenate(
            [taps[f, :, pl.ds((2 - y + first) * COLS, rows * COLS)] for y in range(3)], axis=0
        )

    def finish_out(f, cells, image, conv, cot):
        gain = wide(gains[1], 2 * COLS)
        out = image + conv
        parts = norm_parts(out, gain)
        hh = (parts[2] * parts[3]).astype(BF16)
        grad = norm_pull(parts, gain, cot)
        before = by_row(earlier, grad).astype(BF16)
        after = by_row(later, grad).astype(BF16)
        here = grad.astype(BF16)
        for n, at in enumerate(cells):
            part = slice(n * COLS, (n + 1) * COLS)
            lanes = slice(at * COLS, (at + 1) * COLS)
            head[f + 2, :, lanes] = hh[:, part]
            dout[f, :, lanes] = grad[:, part]
            dob[f, :, lanes] = here[:, part]
            dsh[f, 0:C, lanes] = before[:, part]
            dsh[f, C : 2 * C, lanes] = here[:, part]
            dsh[f, 2 * C : 3 * C, lanes] = after[:, part]

    def columns(z, first, last):
        return z[C : 2 * C] + by_row(first, z[0:C]) + by_row(last, z[2 * C : 3 * C])

    def middle_of(field, f):
        return jnp.concatenate(
            [field[f + t, :, y * COLS : (y + 2) * COLS] for y in range(3) for t in range(3)], axis=0
        )

    def edges_of(field, top, bottom, f):
        parts = []
        for y in range(3):
            for t in range(3):
                one = top[f + t] if y == 0 else field[f + t, :, (y - 1) * COLS : y * COLS]
                two = bottom[f + t] if y == 2 else field[f + t, :, (y + 2) * COLS : (y + 3) * COLS]
                parts.append(jnp.concatenate([one, two], axis=1))
        return jnp.concatenate(parts, axis=0)

    def forward_middle(f, carry):
        conv = columns(dot(wf[...], middle_of(hin, f)), later, earlier)
        cot = dot(hwt[...], pixel_taps(f + 2, 1, 2))
        finish_out(f, (1, 2), xs[f, :, COLS : 3 * COLS], conv, cot)
        return carry

    lax.fori_loop(0, FR, forward_middle, 0)

    def hin_arrived(f):
        for side in range(2):
            hin_copy(side, f).wait_recv()

        @pl.when(me == 0)
        def _():
            hin_t[f] = jnp.zeros((C, COLS), BF16)

        @pl.when(me == slabs - 1)
        def _():
            hin_b[f] = jnp.zeros((C, COLS), BF16)

    hin_arrived(0)
    hin_arrived(1)

    def forward_edges(f, carry):
        hin_arrived(f + 2)
        conv = columns(dot(wf[...], edges_of(hin, hin_t, hin_b, f)), later, earlier)
        window = jnp.concatenate([pixel_taps(f + 2, 0, 1), pixel_taps(f + 2, 3, 1)], axis=1)
        cot = dot(hwt[...], window)
        image = jnp.concatenate([xs[f, :, 0:COLS], xs[f, :, 3 * COLS : 4 * COLS]], axis=1)
        finish_out(f, (0, 3), image, conv, cot)
        for side in range(2):
            dob_copy(side, f).start()
        return carry

    lax.fori_loop(0, FR, forward_edges, 0)

    def main_grad(f, carry):
        parts = []
        for y in range(3):
            for t in range(3):
                if y == 0:
                    block = jnp.concatenate([hin_t[f + t], hin[f + t, :, 0 : 3 * COLS]], axis=1)
                elif y == 1:
                    block = hin[f + t]
                else:
                    block = jnp.concatenate([hin[f + t, :, COLS : 4 * COLS], hin_b[f + t]], axis=1)
                parts.append(block)
        grads[:, 0:K3] += dot_nt(dsh[f], jnp.concatenate(parts, axis=0))
        return carry

    grads[...] = jnp.zeros_like(grads)
    lax.fori_loop(0, FR, main_grad, 0)

    def head_grad(f, total):
        return total + dot_nt(pixel_taps(f, 0, 4), head[f])

    head_total = lax.fori_loop(0, 8, head_grad, jnp.zeros((C, C), F32))
    for x in range(3):
        grads[x * C : (x + 1) * C, K3 : K3 + 32] = head_total[:, 32 * x : 32 * (x + 1)]

    per = TILES // 2 // planes
    for tile in range(TILES):
        half, rest = divmod(tile, TILES // 2)
        owner, k = divmod(rest, per)
        row, lane = divmod(tile, 7)
        if row < 18:
            value = grads[row * 16 : (row + 1) * 16, lane * COLS : (lane + 1) * COLS].astype(BF16)
        else:
            value = jnp.zeros((16, COLS), BF16)
        piece[half, owner, k * 16 : (k + 1) * 16, :] = value

    def pair_copy():
        return remote(piece.at[1 - core], got1, s1, r1, sibling)

    def scatter_copy(k):
        return remote(sum1.at[(xy + k) % planes], got2.at[k], s2.at[k], r2.at[k], in_plane(k))

    def z_copy():
        return remote(half3, got3, s3, r3, zpartner)

    def gather_copy(k):
        return remote(full.at[core, xy], full.at[core, xy], s4.at[k], r4.at[k], in_plane(k))

    def forward_copy(k):
        at = (xy + planes - k) % planes
        return remote(full.at[core, at], full.at[core, at], s5.at[k], r5.at[k], sibling)

    pair_copy().start()

    dob[6] = jnp.zeros((C, 4 * COLS), BF16)
    dob[7] = jnp.zeros((C, 4 * COLS), BF16)
    for f in (6, 7):
        dob_t[f] = jnp.zeros((C, COLS), BF16)
        dob_b[f] = jnp.zeros((C, COLS), BF16)

    def finish_in(f, cells, conv):
        gain = wide(gains[0], 2 * COLS)
        lanes = [slice(at * COLS, (at + 1) * COLS) for at in cells]
        image = jnp.concatenate([xs[f, :, at] for at in lanes], axis=1)
        grad = norm_pull(norm_parts(image, gain), gain, conv)
        for n, at in enumerate(cells):
            value = grad[:, n * COLS : (n + 1) * COLS] + dout[f, :, lanes[n]]
            gi_ref[f, pl.ds(at, C, stride=4), :] = value

    def backward_middle(f, carry):
        finish_in(f, (1, 2), columns(dot(wt[...], middle_of(dob, f)), earlier, later))
        return carry

    def backward_edges(f, carry):
        window = edges_of(dob, dob_t, dob_b, f)
        finish_in(f, (0, 3), columns(dot(wt[...], window), earlier, later))
        return carry

    lax.fori_loop(0, 2, backward_middle, 0)

    pair_copy().wait_recv()
    sum1[...] = (piece[core].astype(F32) + got1[...].astype(F32)).astype(BF16)

    def start_scatter(k, carry):
        scatter_copy(k).start()
        return carry

    lax.fori_loop(1, planes, start_scatter, 0)
    lax.fori_loop(2, FR, backward_middle, 0)

    def add_piece(k, total):
        scatter_copy(k).wait_recv()
        return total + got2[k].astype(F32)

    mine = lax.fori_loop(1, planes, add_piece, sum1[xy].astype(F32))
    half3[...] = mine.astype(BF16)
    z_copy().start()

    for f in range(FR):
        for side in range(2):
            dob_copy(side, f).wait_recv()

    @pl.when(me == 0)
    def _():
        dob_t[0:FR] = jnp.zeros((FR, C, COLS), BF16)

    @pl.when(me == slabs - 1)
    def _():
        dob_b[0:FR] = jnp.zeros((FR, C, COLS), BF16)

    lax.fori_loop(0, 2, backward_edges, 0)

    z_copy().wait_recv()
    full[core, xy] = (half3[...].astype(F32) + got3[...].astype(F32)).astype(BF16)

    def start_gather(k, carry):
        gather_copy(k).start()
        return carry

    forward_copy(0).start()
    lax.fori_loop(1, planes, start_gather, 0)
    lax.fori_loop(2, FR, backward_edges, 0)

    def pass_on(k, carry):
        gather_copy(k).wait_recv()
        forward_copy(k).start()
        return carry

    lax.fori_loop(1, planes, pass_on, 0)

    def passed_on(k, carry):
        forward_copy(k).wait_recv()
        return carry

    lax.fori_loop(0, planes, passed_on, 0)

    scale = (1.0 / (FR * slabs * 4 * COLS)) ** 0.5
    for tile in range(18 * 7):
        half, rest = divmod(tile, TILES // 2)
        owner, k = divmod(rest, per)
        row, lane = divmod(tile, 7)
        value = full[half, owner, k * 16 : (k + 1) * 16, :].astype(F32) * scale
        grads[row * 16 : (row + 1) * 16, lane * COLS : (lane + 1) * COLS] = value
    for x in range(3):
        for y in range(3):
            for t in range(3):
                at = (y * 3 + t) * C
                gm_ref[t, y, x] = grads[x * C : (x + 1) * C, at : at + C]
    head_total = jnp.concatenate(
        [grads[x * C : (x + 1) * C, K3 : K3 + 32] for x in range(3)], axis=1
    )
    for y in range(3):
        for x in range(3):
            for t in range(3):
                at = y * 32 + x * 9 + t * 3
                gh_ref[2 - t, y, x] = head_total[at : at + 3, :]

    for side in range(2):
        pg_copy(side).wait_send()

    def hin_left(f, carry):
        for side in range(2):
            hin_copy(side, f).wait_send()
        return carry

    lax.fori_loop(0, 8, hin_left, 0)

    def dob_left(f, carry):
        for side in range(2):
            dob_copy(side, f).wait_send()
        return carry

    lax.fori_loop(0, FR, dob_left, 0)
    pair_copy().wait_send()
    z_copy().wait_send()
    forward_copy(0).wait_send()

    def sums_left(k, carry):
        scatter_copy(k).wait_send()
        gather_copy(k).wait_send()
        forward_copy(k).wait_send()
        return carry

    lax.fori_loop(1, planes, sums_left, 0)


def local(slabs, *operands):
    (x, mc, hc, gin, gout, mw, hw, ag, tab, idx, order) = operands
    planes = slabs // 4
    piece = (planes, 1024 // planes, COLS)
    vmem = pl.BlockSpec(memory_space=pltpu.VMEM)
    smem = pl.BlockSpec(memory_space=pltpu.SMEM)
    dma = pltpu.SemaphoreType.DMA
    gi, gm, gh = pl.pallas_call(
        functools.partial(kernel, slabs),
        out_shape=(
            jax.ShapeDtypeStruct((FR, 4 * C, COLS), F32),
            jax.ShapeDtypeStruct((3, 3, 3, C, C), F32),
            jax.ShapeDtypeStruct((3, 3, 3, 3, C), F32),
        ),
        in_specs=[vmem] * 8 + [smem] * 3,
        out_specs=[vmem] * 3,
        scratch_shapes=[
            pltpu.VMEM((FR, 4 * C, COLS), F32),
            pltpu.VMEM((FR, C, 4 * COLS), F32),
            pltpu.VMEM((2, C, COLS), F32),
            pltpu.VMEM((8, C, 4 * COLS), BF16),
            pltpu.VMEM((8, C, COLS), BF16),
            pltpu.VMEM((8, C, COLS), BF16),
            pltpu.VMEM((8, C, 4 * COLS), BF16),
            pltpu.VMEM((2, 3 * C, 7 * COLS), F32),
            pltpu.VMEM((3 * C, K3), BF16),
            pltpu.VMEM((3 * C, K3), BF16),
            pltpu.VMEM((C, C), BF16),
            pltpu.VMEM((4, 32, COLS), F32),
            pltpu.VMEM((4, 32, COLS), BF16),
            pltpu.VMEM((2, 32, COLS), BF16),
            pltpu.VMEM((8, 32, 6 * COLS), BF16),
            pltpu.VMEM((FR, C, 4 * COLS), F32),
            pltpu.VMEM((8, C, 4 * COLS), BF16),
            pltpu.VMEM((8, C, COLS), BF16),
            pltpu.VMEM((8, C, COLS), BF16),
            pltpu.VMEM((FR, 3 * C, 4 * COLS), BF16),
            pltpu.VMEM((3 * C, 7 * COLS), F32),
            pltpu.VMEM((2,) + piece, BF16),
            pltpu.VMEM(piece, BF16),
            pltpu.VMEM(piece, BF16),
            pltpu.VMEM(piece, BF16),
            pltpu.VMEM(piece[1:], BF16),
            pltpu.VMEM(piece[1:], BF16),
            pltpu.VMEM((2,) + piece, BF16),
            dma((2, 8)),
            dma((2, 8)),
            dma((2,)),
            dma((2,)),
            dma((2, FR)),
            dma((2, FR)),
            dma,
            dma,
            dma((planes,)),
            dma((planes,)),
            dma,
            dma,
            dma((planes,)),
            dma((planes,)),
            dma((planes,)),
            dma((planes,)),
        ],
        compiler_params=pltpu.CompilerParams(
            collective_id=0, has_side_effects=True, vmem_limit_bytes=56 * 2**20
        ),
    )(
        x.reshape(FR, 4 * C, COLS),
        mc.reshape(2, 4 * C, COLS),
        hc.reshape(2, 4 * C, COLS),
        gin.reshape(1, C),
        gout.reshape(1, C),
        mw,
        hw,
        ag,
        tab,
        idx,
        order,
    )
    return gi.reshape(FR, C, 4, COLS), gm, gh


def solution(mesh):
    tile = P("video", None, "slab", None)
    whole = P("video", None, None, None, None)
    placed = (tile, tile, tile, P(), P(), P(), P(), tile, P(), P("video"), P())
    return jax.shard_map(
        functools.partial(local, mesh.shape["slab"]),
        mesh=mesh,
        in_specs=placed,
        out_specs=(tile, whole, whole),
        check_vma=False,
    )
```

```python
import functools

import jax
import jax.numpy as jnp
from jax import lax
from jax.experimental import pallas as pl
from jax.experimental.pallas import tpu as pltpu
from jax.sharding import PartitionSpec as P

EPS = 1e-06
MESH = pl.DeviceIdType.MESH
F32 = jnp.float32
BF16 = jnp.bfloat16
C = 96
FR = 6
COLS = 128
K3 = 9 * C


def dot(a, b):
    return lax.dot_general(a, b, (((1,), (0,)), ((), ())), preferred_element_type=F32)


def dot_nt(a, b):
    return lax.dot_general(a, b, (((1,), (1,)), ((), ())), preferred_element_type=F32)


def lane_of(value):
    return lax.broadcasted_iota(jnp.int32, value.shape, 1)


def later(value):
    return jnp.where(lane_of(value) == 0, 0.0, pltpu.roll(value, 1, 1))


def earlier(value):
    return jnp.where(lane_of(value) == COLS - 1, 0.0, pltpu.roll(value, COLS - 1, 1))


def by_row(shift, value):
    parts = [shift(value[:, i : i + COLS]) for i in range(0, value.shape[1], COLS)]
    return jnp.concatenate(parts, axis=1)


def wide(gain, width):
    return jnp.concatenate([gain] * (width // COLS), axis=1)


def norm_parts(value, gain):
    meansq = jnp.sum(value * value, axis=0, keepdims=True) * (1.0 / C)
    root = lax.rsqrt(meansq + EPS)
    unit = value * root
    normed = unit * gain
    sig = 0.5 * jnp.tanh(0.5 * normed) + 0.5
    return root, unit, normed, sig


def norm_pull(parts, gain, cot):
    root, unit, normed, sig = parts
    inner = cot * gain * (sig * (1.0 + normed * (1.0 - sig)))
    mean = jnp.sum(inner * unit, axis=0, keepdims=True) * (1.0 / C)
    return root * (inner - unit * mean)


def kernel(
    slabs,
    x_hbm,
    mc_hbm,
    hc_hbm,
    gin_hbm,
    gout_hbm,
    mw_hbm,
    hw_hbm,
    ag_hbm,
    tab_hbm,
    idx_hbm,
    ord_hbm,
    gi_hbm,
    sums_hbm,
    x_ref,
    mc_ref,
    hc_ref,
    gin_ref,
    gout_ref,
    mw_ref,
    hw_ref,
    ag_ref,
    tab_ref,
    idx_ref,
    ord_ref,
    gi_ref,
    stage,
    xs,
    gains,
    hin,
    hin_t,
    hin_b,
    head,
    wtmp,
    wf,
    wt,
    hwt,
    pg_own,
    pg_send,
    pg_halo,
    taps,
    dout,
    dob,
    dob_t,
    dob_b,
    dsh_mid,
    dsh_edge,
    mid_grads,
    head_mid,
    head_sum,
    grads,
    piece,
    got1,
    sum1,
    got2,
    half3,
    got3,
    full,
    ins,
    outs,
    hs,
    hr,
    ps,
    pr,
    ds,
    dr,
    s1,
    r1,
    s2,
    r2,
    s3,
    r3,
    s4,
    r4,
    s5,
    r5,
):
    me = lax.axis_index("slab")
    core = me % 2
    place = me % 4
    zh = place // 2
    xy = me // 4
    planes = slabs // 4
    up = (me + slabs - 1) % slabs
    down = (me + 1) % slabs
    sibling = me + 1 - 2 * core
    zpartner = me + 2 - 4 * zh

    def in_plane(k):
        return ((xy + k) % planes) * 4 + place

    pairs = (
        (x_hbm, x_ref),
        (mc_hbm, mc_ref),
        (hc_hbm, hc_ref),
        (gin_hbm, gin_ref),
        (gout_hbm, gout_ref),
        (mw_hbm, mw_ref),
        (hw_hbm, hw_ref),
        (ag_hbm, ag_ref),
        (tab_hbm, tab_ref),
        (idx_hbm, idx_ref),
        (ord_hbm, ord_ref),
    )
    loads = [pltpu.make_async_copy(a, b, ins.at[n]) for n, (a, b) in enumerate(pairs)]

    def remote(src, dst, send, recv, to):
        return pltpu.make_async_remote_copy(
            src_ref=src,
            dst_ref=dst,
            send_sem=send,
            recv_sem=recv,
            device_id={"slab": to},
            device_id_type=MESH,
        )

    barrier = pltpu.get_barrier_semaphore()

    def greet(to):
        pl.semaphore_signal(barrier, inc=1, device_id={"slab": to}, device_id_type=MESH)

    greet(up)
    greet(down)
    greet(zpartner)
    for k in range(1, planes):
        greet(in_plane(k))
    for n in (1, 0, 3, 8, 9, 10, 7, 2, 5, 6, 4):
        loads[n].start()

    def split_rows(f, source):
        stage[f] = source.astype(F32)
        return jnp.concatenate(
            [stage[f, pl.ds(r, C, stride=4), :] for r in range(4)], axis=1
        )

    loads[1].wait()
    for j in range(2):
        hin[j] = split_rows(j, mc_ref[j]).astype(BF16)

    def pg_copy(side):
        return remote(
            pg_send.at[0 if side == 0 else 3],
            pg_halo.at[1 - side],
            ps.at[side],
            pr.at[1 - side],
            up if side == 0 else down,
        )

    def hin_copy(side, f):
        if side == 0:
            return remote(hin.at[f, :, pl.ds(0, COLS)], hin_b.at[f], hs.at[0, f], hr.at[1, f], up)
        return remote(hin.at[f, :, pl.ds(3 * COLS, COLS)], hin_t.at[f], hs.at[1, f], hr.at[0, f], down)

    def dob_copy(side, f):
        if side == 0:
            return remote(dob.at[f, :, pl.ds(0, COLS)], dob_b.at[f], ds.at[0, f], dr.at[1, f], up)
        return remote(dob.at[f, :, pl.ds(3 * COLS, COLS)], dob_t.at[f], ds.at[1, f], dr.at[0, f], down)

    for n in (7, 8, 9, 10):
        loads[n].wait()
    pg_own[...] = jnp.zeros_like(pg_own)
    for f in range(FR):
        picked = []
        for a in range(4):
            total = None
            for j in range(FR):
                weight = jnp.where(ord_ref[j] == f, 1.0, 0.0).astype(F32)
                term = ag_ref[j, a].astype(F32) * weight
                total = term if total is None else total + term
            picked.append(total)
        row = idx_ref[f]
        for c in range(3):
            value = picked[0] * tab_ref[c, 0, row]
            for a in range(1, 4):
                value = value + picked[a] * tab_ref[c, a, row]
            for r in range(4):
                pg_own[r, 6 + 3 * f + c : 7 + 3 * f + c, :] = value[r : r + 1, :]
    pg_send[...] = pg_own[...].astype(BF16)
    loads[0].wait()
    loads[3].wait()
    gains[0] = jnp.broadcast_to(gin_ref[...], (COLS, C)).T
    pl.semaphore_wait(barrier, planes + 2)
    for side in range(2):
        pg_copy(side).start()
    for j in range(2):
        for side in range(2):
            hin_copy(side, j).start()

    def make_h(f):
        value = split_rows(f, x_ref[f])
        xs[f] = value
        _, _, normed, sig = norm_parts(value, wide(gains[0], 4 * COLS))
        hin[f + 2] = (normed * sig).astype(BF16)
        for side in range(2):
            hin_copy(side, f + 2).start()

    for f in range(0, FR):
        make_h(f)

    loads[4].wait()
    gains[1] = jnp.broadcast_to(gout_ref[...], (COLS, C)).T

    loads[5].wait()
    for x in range(3):
        for y in range(3):
            for t in range(3):
                at = (y * 3 + t) * C
                wtmp[0, x * C : (x + 1) * C, at : at + C] = mw_ref[t, y, x].astype(F32)
                wtmp[1, x * C : (x + 1) * C, at : at + C] = mw_ref[2 - t, 2 - y, x].astype(F32).T
    wf[...] = wtmp[0, :, 0:K3].astype(BF16)
    wt[...] = wtmp[1, :, 0:K3].astype(BF16)
    loads[6].wait()
    grads[0:C, 0:C] = jnp.zeros((C, C), F32)
    for y in range(3):
        for x in range(3):
            for t in range(3):
                at = y * 32 + x * 9 + t * 3
                grads[at : at + 3, 0:C] = hw_ref[2 - t, y, x].astype(F32)
    hwt[...] = grads[0:C, 0:C].T.astype(BF16)
    loads[2].wait()
    for j in range(2):
        head[j] = split_rows(j, hc_ref[j]).astype(BF16)

    out_row = lax.broadcasted_iota(jnp.int32, (8 * 32, C), 0)
    in_row = lax.broadcasted_iota(jnp.int32, (8 * 32, C), 1)
    frame = lax.shift_right_logical(out_row, 5)
    tap = out_row - 32 * frame
    col = jnp.where(tap >= 9, 1, 0) + jnp.where(tap >= 18, 1, 0)
    source = col * 32 + frame * 3 + (tap - 9 * col)
    chosen = jnp.where((in_row == source) & (tap < 27), 1.0, 0.0).astype(BF16)

    def spread(rows, lanes):
        rows = [value.astype(F32) for value in rows]
        stack = jnp.concatenate(
            [
                jnp.concatenate([earlier(value) for value in rows], axis=1),
                jnp.concatenate(rows, axis=1),
                jnp.concatenate([later(value) for value in rows], axis=1),
            ],
            axis=0,
        )
        result = dot(chosen, stack.astype(BF16)).astype(BF16)
        for f in range(8):
            for n, at in enumerate(lanes):
                value = result[f * 32 : (f + 1) * 32, n * COLS : (n + 1) * COLS]
                taps[f, :, at * COLS : (at + 1) * COLS] = value

    spread([pg_send[r] for r in range(4)], (1, 2, 3, 4))

    def pixel_taps(f, first, rows):
        return jnp.concatenate(
            [taps[f, :, pl.ds((2 - y + first) * COLS, rows * COLS)] for y in range(3)], axis=0
        )

    def finish_out(f, cells, image, conv, cot, shifted):
        gain = wide(gains[1], 2 * COLS)
        out = image + conv
        parts = norm_parts(out, gain)
        hh = (parts[2] * parts[3]).astype(BF16)
        grad = norm_pull(parts, gain, cot)
        before = by_row(earlier, grad).astype(BF16)
        after = by_row(later, grad).astype(BF16)
        here = grad.astype(BF16)
        for n, at in enumerate(cells):
            part = slice(n * COLS, (n + 1) * COLS)
            lanes = slice(at * COLS, (at + 1) * COLS)
            head[f + 2, :, lanes] = hh[:, part]
            dout[f, :, lanes] = grad[:, part]
            dob[f, :, lanes] = here[:, part]
        shifted[0, f, 0:C] = before
        shifted[0, f, C : 3 * C // 2] = here[0 : C // 2]
        shifted[1, f, 0 : C // 2] = here[C // 2 : C]
        shifted[1, f, C // 2 : 3 * C // 2] = after

    def columns(z, first, last):
        return z[C : 2 * C] + by_row(first, z[0:C]) + by_row(last, z[2 * C : 3 * C])

    def middle_of(field, f):
        return jnp.concatenate(
            [field[f + t, :, y * COLS : (y + 2) * COLS] for y in range(3) for t in range(3)], axis=0
        )

    def edges_of(field, top, bottom, f):
        parts = []
        for y in range(3):
            for t in range(3):
                one = top[f + t] if y == 0 else field[f + t, :, (y - 1) * COLS : y * COLS]
                two = bottom[f + t] if y == 2 else field[f + t, :, (y + 2) * COLS : (y + 3) * COLS]
                parts.append(jnp.concatenate([one, two], axis=1))
        return jnp.concatenate(parts, axis=0)

    def forward_middle(f):
        conv = columns(dot(wf[...], middle_of(hin, f)), later, earlier)
        cot = dot(hwt[...], pixel_taps(f + 2, 1, 2))
        finish_out(f, (1, 2), xs[f, :, COLS : 3 * COLS], conv, cot, dsh_mid)

    for f in range(0, FR):
        forward_middle(f)

    def edge_windows(frames):
        return jnp.concatenate([edges_of(hin, hin_t, hin_b, f) for f in frames], axis=1)

    def edge_grads(half, frames):
        return jnp.concatenate([dsh_edge[half, f] for f in frames], axis=1)

    shifted = [
        jnp.concatenate([dsh_mid[half, f] for f in range(FR)], axis=1) for half in range(2)
    ]
    middle = dot_nt(
        jnp.concatenate(shifted, axis=0),
        jnp.concatenate([middle_of(hin, f) for f in range(FR)], axis=1),
    )
    mid_grads[0] = middle[0 : 3 * C // 2]
    mid_grads[1] = middle[3 * C // 2 : 3 * C]

    def head_edge_taps(f):
        return jnp.concatenate([pixel_taps(f, 0, 1), pixel_taps(f, 3, 1)], axis=1)

    def head_edges(f):
        return jnp.concatenate([head[f, :, 0:COLS], head[f, :, 3 * COLS : 4 * COLS]], axis=1)

    head_mid[...] = dot_nt(
        jnp.concatenate([pixel_taps(f, 1, 2) for f in range(8)], axis=1),
        jnp.concatenate([head[f, :, COLS : 3 * COLS] for f in range(8)], axis=1),
    )

    def hin_arrived(frames):
        for f in frames:
            for side in range(2):
                hin_copy(side, f).wait_recv()

        some = slice(frames[0], frames[-1] + 1)
        shape = (len(frames), C, COLS)

        @pl.when(me == 0)
        def _():
            hin_t[some] = jnp.zeros(shape, BF16)

        @pl.when(me == slabs - 1)
        def _():
            hin_b[some] = jnp.zeros(shape, BF16)

    for side in range(2):
        pg_copy(side).wait_recv()

    @pl.when(me == 0)
    def _():
        pg_halo[0] = jnp.zeros((32, COLS), BF16)

    @pl.when(me == slabs - 1)
    def _():
        pg_halo[1] = jnp.zeros((32, COLS), BF16)

    spread([pg_halo[0], pg_halo[1]], (0, 5))

    def forward_edges(f):
        conv = columns(dot(wf[...], edges_of(hin, hin_t, hin_b, f)), later, earlier)
        cot = dot(hwt[...], head_edge_taps(f + 2))
        image = jnp.concatenate([xs[f, :, 0:COLS], xs[f, :, 3 * COLS : 4 * COLS]], axis=1)
        finish_out(f, (0, 3), image, conv, cot, dsh_edge)

    early = range(0, 4)
    late = range(4, FR)
    hin_arrived(range(0, 6))
    for f in early:
        forward_edges(f)
    for f in early:
        for side in range(2):
            dob_copy(side, f).start()
    part = dot_nt(
        jnp.concatenate([edge_grads(0, early), edge_grads(1, early)], axis=0), edge_windows(early)
    )
    mid_grads[0] += part[0 : 3 * C // 2]
    mid_grads[1] += part[3 * C // 2 : 3 * C]
    hin_arrived(range(6, 8))
    for f in late:
        forward_edges(f)
    for f in late:
        for side in range(2):
            dob_copy(side, f).start()

    total = head_mid[...] + dot_nt(
        jnp.concatenate([head_edge_taps(f) for f in range(8)], axis=1),
        jnp.concatenate([head_edges(f) for f in range(8)], axis=1),
    )
    head_sum[0] = total[0 : C // 2]
    head_sum[1] = total[C // 2 : C]

    per = 64 // planes

    def where_is(tile):
        owner, k = divmod(tile, per)
        return owner, slice(k * 16, (k + 1) * 16)

    def tile_of(tile):
        row, lane = divmod(tile, 7)
        return grads[row * 16 : (row + 1) * 16, lane * COLS : (lane + 1) * COLS]

    def half_grads(half):
        grads[:, 0:K3] = mid_grads[half] + dot_nt(edge_grads(half, late), edge_windows(late))
        for n in range(3):
            rows = slice(n * (C // 2), (n + 1) * (C // 2))
            grads[rows, K3 : K3 + 32] = head_sum[half, :, n * 32 : (n + 1) * 32]

    def pair_copy():
        return remote(piece, got1, s1, r1, sibling)

    def scatter_copy(k):
        return remote(sum1.at[(xy + k) % planes], got2.at[k], s2.at[k], r2.at[k], in_plane(k))

    def z_copy():
        return remote(half3, got3, s3, r3, zpartner)

    def gather_copy(k):
        mine = full.at[core, xy]
        return remote(mine, mine, s4.at[k], r4.at[k], in_plane(k))

    def pass_on(k):
        one = full.at[core, (xy + planes - k) % planes]
        return remote(one, one, s5.at[k], r5.at[k], sibling)

    half_grads(1 - core)
    for tile in range(64):
        owner, rows = where_is(tile)
        value = tile_of(tile).astype(BF16) if tile < 63 else jnp.zeros((16, COLS), BF16)
        piece[owner, rows] = value
    pair_copy().start()
    half_grads(core)

    dob[6] = jnp.zeros((C, 4 * COLS), BF16)
    dob[7] = jnp.zeros((C, 4 * COLS), BF16)
    for f in (6, 7):
        dob_t[f] = jnp.zeros((C, COLS), BF16)
        dob_b[f] = jnp.zeros((C, COLS), BF16)

    def finish_in(f, cells, conv):
        gain = wide(gains[0], 2 * COLS)
        lanes = [slice(at * COLS, (at + 1) * COLS) for at in cells]
        image = jnp.concatenate([xs[f, :, at] for at in lanes], axis=1)
        grad = norm_pull(norm_parts(image, gain), gain, conv)
        for n, at in enumerate(cells):
            value = grad[:, n * COLS : (n + 1) * COLS] + dout[f, :, lanes[n]]
            gi_ref[f, pl.ds(at, C, stride=4), :] = value

    def backward_middle(f):
        finish_in(f, (1, 2), columns(dot(wt[...], middle_of(dob, f)), earlier, later))

    def backward_edges(f):
        window = edges_of(dob, dob_t, dob_b, f)
        finish_in(f, (0, 3), columns(dot(wt[...], window), earlier, later))

    pair_copy().wait_recv()
    for tile in range(64):
        owner, rows = where_is(tile)
        value = got1[owner, rows].astype(F32)
        if tile < 63:
            value = value + tile_of(tile)
        sum1[owner, rows] = value.astype(BF16)
    for k in range(1, planes):
        scatter_copy(k).start()

    for f in range(0, FR):
        backward_middle(f)

    total = sum1[xy].astype(F32)
    for k in range(1, planes):
        scatter_copy(k).wait_recv()
    for k in range(1, planes):
        total = total + got2[k].astype(F32)
    half3[...] = total.astype(BF16)
    z_copy().start()

    for f in range(FR):
        for side in range(2):
            dob_copy(side, f).wait_recv()

    @pl.when(me == 0)
    def _():
        dob_t[0:FR] = jnp.zeros((FR, C, COLS), BF16)

    @pl.when(me == slabs - 1)
    def _():
        dob_b[0:FR] = jnp.zeros((FR, C, COLS), BF16)

    for f in range(0, FR):
        backward_edges(f)
    store = pltpu.make_async_copy(gi_ref, gi_hbm, outs.at[0])
    store.start()

    z_copy().wait_recv()
    full[core, xy] = (half3[...].astype(F32) + got3[...].astype(F32)).astype(BF16)
    for k in range(1, planes):
        gather_copy(k).start()
    pass_on(0).start()
    for k in range(1, planes):
        gather_copy(k).wait_recv()
        pass_on(k).start()
    own = pltpu.make_async_copy(full.at[core], sums_hbm.at[core], outs.at[1])
    own.start()
    for k in range(planes):
        pass_on(k).wait_recv()
    other = pltpu.make_async_copy(full.at[1 - core], sums_hbm.at[1 - core], outs.at[2])
    other.start()

    for side in range(2):
        pg_copy(side).wait_send()
        for f in range(8):
            hin_copy(side, f).wait_send()
        for f in range(FR):
            dob_copy(side, f).wait_send()
    pair_copy().wait_send()
    z_copy().wait_send()
    pass_on(0).wait_send()
    for k in range(1, planes):
        scatter_copy(k).wait_send()
        gather_copy(k).wait_send()
        pass_on(k).wait_send()
    store.wait()
    own.wait()
    other.wait()


def finish(slabs, gi_hbm, sums_hbm, out_hbm, gm_hbm, gh_ref, gi, sums, grads, gm, ins, outs):
    sums_in = pltpu.make_async_copy(sums_hbm, sums, ins.at[FR])
    sums_in.start()
    gi_in = [pltpu.make_async_copy(gi_hbm.at[f], gi.at[f], ins.at[f]) for f in range(FR)]
    gi_out = [pltpu.make_async_copy(gi.at[f], out_hbm.at[f], outs.at[f]) for f in range(FR)]
    for copy in gi_in:
        copy.start()
    planes = slabs // 4
    per = 64 // planes
    scale = (1.0 / (FR * slabs * 4 * COLS)) ** 0.5
    sums_in.wait()
    for half in range(2):
        for tile in range(63):
            owner, k = divmod(tile, per)
            row, lane = divmod(tile, 7)
            at = half * (3 * C // 2) + row * 16
            value = sums[half, owner, k * 16 : (k + 1) * 16].astype(F32) * scale
            grads[at : at + 16, lane * COLS : (lane + 1) * COLS] = value
    for f in range(FR):
        gi_in[f].wait()
        gi_out[f].start()
    gm_out = []
    for t in range(3):
        for y in range(3):
            for x in range(3):
                at = (y * 3 + t) * C
                gm[t, y, x] = grads[x * C : (x + 1) * C, at : at + C]
        gm_out.append(pltpu.make_async_copy(gm.at[t], gm_hbm.at[t], outs.at[FR + t]))
        gm_out[t].start()
    head = []
    for half in range(2):
        top = half * (3 * C // 2)
        parts = [
            grads[top + n * (C // 2) : top + (n + 1) * (C // 2), K3 : K3 + 32] for n in range(3)
        ]
        head.append(jnp.concatenate(parts, axis=1))
    head = jnp.concatenate(head, axis=0)
    for y in range(3):
        for x in range(3):
            for t in range(3):
                at = y * 32 + x * 9 + t * 3
                gh_ref[2 - t, y, x] = head[at : at + 3, :]
    for copy in gi_out + gm_out:
        copy.wait()


def local(slabs, *operands):
    (x, mc, hc, gin, gout, mw, hw, ag, tab, idx, order) = operands
    planes = slabs // 4
    unit = (1024 // planes, COLS)
    plane = (planes,) + unit
    anywhere = pl.BlockSpec(memory_space=pl.ANY)
    hbm = pl.BlockSpec(memory_space=pltpu.HBM)
    vmem = pl.BlockSpec(memory_space=pltpu.VMEM)
    dma = pltpu.SemaphoreType.DMA
    operands = (
        x.reshape(FR, 4 * C, COLS),
        mc.reshape(2, 4 * C, COLS),
        hc.reshape(2, 4 * C, COLS),
        gin.reshape(1, C),
        gout.reshape(1, C),
        mw,
        hw,
        ag,
        jnp.transpose(tab, (1, 2, 0)),
        idx,
        order,
    )
    gi_shape = jax.ShapeDtypeStruct((FR, 4 * C, COLS), F32)
    gi, sums = pl.pallas_call(
        functools.partial(kernel, slabs),
        out_shape=(gi_shape, jax.ShapeDtypeStruct((2,) + plane, BF16)),
        in_specs=[anywhere] * 11,
        out_specs=[anywhere] * 2,
        scratch_shapes=[pltpu.VMEM(value.shape, value.dtype) for value in operands[:8]]
        + [pltpu.SMEM(value.shape, value.dtype) for value in operands[8:]]
        + [
            pltpu.VMEM((FR, 4 * C, COLS), F32),
            pltpu.VMEM((FR, 4 * C, COLS), F32),
            pltpu.VMEM((FR, C, 4 * COLS), F32),
            pltpu.VMEM((2, C, COLS), F32),
            pltpu.VMEM((8, C, 4 * COLS), BF16),
            pltpu.VMEM((8, C, COLS), BF16),
            pltpu.VMEM((8, C, COLS), BF16),
            pltpu.VMEM((8, C, 4 * COLS), BF16),
            pltpu.VMEM((2, 3 * C, 7 * COLS), F32),
            pltpu.VMEM((3 * C, K3), BF16),
            pltpu.VMEM((3 * C, K3), BF16),
            pltpu.VMEM((C, C), BF16),
            pltpu.VMEM((4, 32, COLS), F32),
            pltpu.VMEM((4, 32, COLS), BF16),
            pltpu.VMEM((2, 32, COLS), BF16),
            pltpu.VMEM((8, 32, 6 * COLS), BF16),
            pltpu.VMEM((FR, C, 4 * COLS), F32),
            pltpu.VMEM((8, C, 4 * COLS), BF16),
            pltpu.VMEM((8, C, COLS), BF16),
            pltpu.VMEM((8, C, COLS), BF16),
            pltpu.VMEM((2, FR, 3 * C // 2, 2 * COLS), BF16),
            pltpu.VMEM((2, FR, 3 * C // 2, 2 * COLS), BF16),
            pltpu.VMEM((2, 3 * C // 2, K3), F32),
            pltpu.VMEM((C, C), F32),
            pltpu.VMEM((2, C // 2, C), F32),
            pltpu.VMEM((3 * C // 2, 7 * COLS), F32),
            pltpu.VMEM(plane, BF16),
            pltpu.VMEM(plane, BF16),
            pltpu.VMEM(plane, BF16),
            pltpu.VMEM(plane, BF16),
            pltpu.VMEM(unit, BF16),
            pltpu.VMEM(unit, BF16),
            pltpu.VMEM((2,) + plane, BF16),
            dma((11,)),
            dma((3,)),
            dma((2, 8)),
            dma((2, 8)),
            dma((2,)),
            dma((2,)),
            dma((2, FR)),
            dma((2, FR)),
            dma,
            dma,
            dma((planes,)),
            dma((planes,)),
            dma,
            dma,
            dma((planes,)),
            dma((planes,)),
            dma((planes,)),
            dma((planes,)),
        ],
        compiler_params=pltpu.CompilerParams(
            collective_id=0, has_side_effects=True, vmem_limit_bytes=56 * 2**20
        ),
    )(*operands)
    gi, gm, gh = pl.pallas_call(
        functools.partial(finish, slabs),
        out_shape=(
            gi_shape,
            jax.ShapeDtypeStruct((3, 3, 3, C, C), F32),
            jax.ShapeDtypeStruct((3, 3, 3, 3, C), F32),
        ),
        in_specs=[hbm, hbm],
        out_specs=[hbm, hbm, vmem],
        scratch_shapes=[
            pltpu.VMEM((FR, 4 * C, COLS), F32),
            pltpu.VMEM((2,) + plane, BF16),
            pltpu.VMEM((3 * C, 7 * COLS), F32),
            pltpu.VMEM((3, 3, 3, C, C), F32),
            dma((FR + 1,)),
            dma((FR + 3,)),
        ],
        compiler_params=pltpu.CompilerParams(vmem_limit_bytes=60 * 2**20),
    )(gi, sums)
    return gi.reshape(FR, C, 4, COLS), gm, gh


def solution(mesh):
    tile = P("video", None, "slab", None)
    whole = P("video", None, None, None, None)
    placed = (tile, tile, tile, P(), P(), P(), P(), tile, P(), P("video"), P())
    return jax.shard_map(
        functools.partial(local, mesh.shape["slab"]),
        mesh=mesh,
        in_specs=placed,
        out_specs=(tile, whole, whole),
        check_vma=False,
    )
```

```python
import functools

import jax
import jax.numpy as jnp
from jax import lax
from jax.experimental import pallas as pl
from jax.experimental.pallas import tpu as pltpu
from jax.sharding import PartitionSpec as P

EPS = 1e-06
MESH = pl.DeviceIdType.MESH
F32 = jnp.float32
BF16 = jnp.bfloat16
C = 96
FR = 6
COLS = 128
K3 = 9 * C


def dot(a, b):
    return lax.dot_general(a, b, (((1,), (0,)), ((), ())), preferred_element_type=F32)


def dot_nt(a, b):
    return lax.dot_general(a, b, (((1,), (1,)), ((), ())), preferred_element_type=F32)


def lane_of(value):
    return lax.broadcasted_iota(jnp.int32, value.shape, 1)


def later(value):
    return jnp.where(lane_of(value) == 0, 0.0, pltpu.roll(value, 1, 1))


def earlier(value):
    return jnp.where(lane_of(value) == COLS - 1, 0.0, pltpu.roll(value, COLS - 1, 1))


def by_row(shift, value):
    parts = [shift(value[:, i : i + COLS]) for i in range(0, value.shape[1], COLS)]
    return jnp.concatenate(parts, axis=1)


def wide(gain, width):
    return jnp.concatenate([gain] * (width // COLS), axis=1)


def norm_parts(value, gain):
    meansq = jnp.sum(value * value, axis=0, keepdims=True) * (1.0 / C)
    root = lax.rsqrt(meansq + EPS)
    unit = value * root
    normed = unit * gain
    sig = 0.5 * jnp.tanh(0.5 * normed) + 0.5
    return root, unit, normed, sig


def norm_pull(parts, gain, cot):
    root, unit, normed, sig = parts
    inner = cot * gain * (sig * (1.0 + normed * (1.0 - sig)))
    mean = jnp.sum(inner * unit, axis=0, keepdims=True) * (1.0 / C)
    return root * (inner - unit * mean)


def kernel(
    slabs,
    x_hbm,
    mc_hbm,
    hc_hbm,
    gin_hbm,
    gout_hbm,
    mw_hbm,
    hw_hbm,
    ag_hbm,
    tab_hbm,
    idx_hbm,
    ord_hbm,
    gi_ref,
    sums_ref,
    x_ref,
    mc_ref,
    hc_ref,
    gin_ref,
    gout_ref,
    mw_ref,
    hw_ref,
    ag_ref,
    tab_ref,
    idx_ref,
    ord_ref,
    stage,
    xs,
    gains,
    hin,
    hin_t,
    hin_b,
    head,
    wtmp,
    wf,
    wt,
    hwt,
    pg_own,
    pg_send,
    pg_halo,
    taps,
    dout,
    dob,
    dob_t,
    dob_b,
    dsh_mid,
    dsh_edge,
    mid_grads,
    head_mid,
    head_sum,
    grads,
    piece,
    got1,
    sum1,
    got2,
    half3,
    got3,
    full,
    ins,
    hs,
    hr,
    ps,
    pr,
    ds,
    dr,
    s1,
    r1,
    s2,
    r2,
    s3,
    r3,
    s4,
    r4,
    s5,
    r5,
):
    me = lax.axis_index("slab")
    core = me % 2
    place = me % 4
    zh = place // 2
    xy = me // 4
    planes = slabs // 4
    up = (me + slabs - 1) % slabs
    down = (me + 1) % slabs
    sibling = me + 1 - 2 * core
    zpartner = me + 2 - 4 * zh

    def in_plane(k):
        return ((xy + k) % planes) * 4 + place

    pairs = (
        (x_hbm, x_ref),
        (mc_hbm, mc_ref),
        (hc_hbm, hc_ref),
        (gin_hbm, gin_ref),
        (gout_hbm, gout_ref),
        (mw_hbm, mw_ref),
        (hw_hbm, hw_ref),
        (ag_hbm, ag_ref),
        (tab_hbm, tab_ref),
        (idx_hbm, idx_ref),
        (ord_hbm, ord_ref),
    )
    loads = [pltpu.make_async_copy(a, b, ins.at[n]) for n, (a, b) in enumerate(pairs)]

    def remote(src, dst, send, recv, to):
        return pltpu.make_async_remote_copy(
            src_ref=src,
            dst_ref=dst,
            send_sem=send,
            recv_sem=recv,
            device_id={"slab": to},
            device_id_type=MESH,
        )

    barrier = pltpu.get_barrier_semaphore()

    def greet(to):
        pl.semaphore_signal(barrier, inc=1, device_id={"slab": to}, device_id_type=MESH)

    greet(up)
    greet(down)
    greet(zpartner)
    for k in range(1, planes):
        greet(in_plane(k))
    for n in (1, 0, 3, 8, 9, 10, 7, 2, 5, 6, 4):
        loads[n].start()

    def split_rows(f, source):
        stage[f] = source.astype(F32)
        return jnp.concatenate(
            [stage[f, pl.ds(r, C, stride=4), :] for r in range(4)], axis=1
        )

    loads[1].wait()
    for j in range(2):
        hin[j] = split_rows(j, mc_ref[j]).astype(BF16)

    def pg_copy(side):
        return remote(
            pg_send.at[0 if side == 0 else 3],
            pg_halo.at[1 - side],
            ps.at[side],
            pr.at[1 - side],
            up if side == 0 else down,
        )

    groups = (slice(0, 4), slice(4, 6), slice(6, 8))

    def hin_copy(side, f):
        group = 0 if f < 4 else 1 if f < 6 else 2
        if side == 0:
            row, there = hin.at[f, :, pl.ds(0, COLS)], hin_b.at[f]
            return remote(row, there, hs.at[0], hr.at[1, group], up)
        row, there = hin.at[f, :, pl.ds(3 * COLS, COLS)], hin_t.at[f]
        return remote(row, there, hs.at[1], hr.at[0, group], down)

    def whole(ref, send, recv):
        return remote(ref, ref, send, recv, sibling)

    def dob_copy(side, f):
        if side == 0:
            row, there = dob.at[f, :, pl.ds(0, COLS)], dob_b.at[f]
            return remote(row, there, ds.at[0], dr.at[1], up)
        row, there = dob.at[f, :, pl.ds(3 * COLS, COLS)], dob_t.at[f]
        return remote(row, there, ds.at[1], dr.at[0], down)

    pl.semaphore_wait(barrier, planes + 2)
    for j in range(2):
        for side in range(2):
            hin_copy(side, j).start()

    for n in (7, 8, 9, 10):
        loads[n].wait()
    pg_own[...] = jnp.zeros_like(pg_own)
    for f in range(FR):
        picked = []
        for a in range(4):
            total = None
            for j in range(FR):
                weight = jnp.where(ord_ref[j] == f, 1.0, 0.0).astype(F32)
                term = ag_ref[j, a].astype(F32) * weight
                total = term if total is None else total + term
            picked.append(total)
        row = idx_ref[f]
        for c in range(3):
            value = picked[0] * tab_ref[c, 0, row]
            for a in range(1, 4):
                value = value + picked[a] * tab_ref[c, a, row]
            for r in range(4):
                pg_own[r, 6 + 3 * f + c : 7 + 3 * f + c, :] = value[r : r + 1, :]
    pg_send[...] = pg_own[...].astype(BF16)
    loads[0].wait()
    loads[3].wait()
    gains[0] = jnp.broadcast_to(gin_ref[...], (COLS, C)).T
    for side in range(2):
        pg_copy(side).start()

    def make_h(f):
        value = split_rows(f, x_ref[f])
        xs[f] = value
        _, _, normed, sig = norm_parts(value, wide(gains[0], 4 * COLS))
        hin[f + 2] = (normed * sig).astype(BF16)
        for side in range(2):
            hin_copy(side, f + 2).start()

    for f in range(0, FR):
        make_h(f)

    loads[4].wait()
    gains[1] = jnp.broadcast_to(gout_ref[...], (COLS, C)).T

    loads[5].wait()
    for x in range(3):
        for y in range(3):
            for t in range(3):
                at = (y * 3 + t) * C
                wtmp[0, x * C : (x + 1) * C, at : at + C] = mw_ref[t, y, x].astype(F32)
                wtmp[1, x * C : (x + 1) * C, at : at + C] = mw_ref[2 - t, 2 - y, x].astype(F32).T
    wf[...] = wtmp[0, :, 0:K3].astype(BF16)
    wt[...] = wtmp[1, :, 0:K3].astype(BF16)
    loads[6].wait()
    grads[0:C, 0:C] = jnp.zeros((C, C), F32)
    for y in range(3):
        for x in range(3):
            for t in range(3):
                at = y * 32 + x * 9 + t * 3
                grads[at : at + 3, 0:C] = hw_ref[2 - t, y, x].astype(F32)
    hwt[...] = grads[0:C, 0:C].T.astype(BF16)
    loads[2].wait()
    for j in range(2):
        head[j] = split_rows(j, hc_ref[j]).astype(BF16)

    out_row = lax.broadcasted_iota(jnp.int32, (8 * 32, C), 0)
    in_row = lax.broadcasted_iota(jnp.int32, (8 * 32, C), 1)
    frame = lax.shift_right_logical(out_row, 5)
    tap = out_row - 32 * frame
    col = jnp.where(tap >= 9, 1, 0) + jnp.where(tap >= 18, 1, 0)
    source = col * 32 + frame * 3 + (tap - 9 * col)
    chosen = jnp.where((in_row == source) & (tap < 27), 1.0, 0.0).astype(BF16)

    def spread(rows, lanes):
        rows = [value.astype(F32) for value in rows]
        stack = jnp.concatenate(
            [
                jnp.concatenate([earlier(value) for value in rows], axis=1),
                jnp.concatenate(rows, axis=1),
                jnp.concatenate([later(value) for value in rows], axis=1),
            ],
            axis=0,
        )
        result = dot(chosen, stack.astype(BF16)).astype(BF16)
        for f in range(8):
            for n, at in enumerate(lanes):
                value = result[f * 32 : (f + 1) * 32, n * COLS : (n + 1) * COLS]
                taps[f, :, at * COLS : (at + 1) * COLS] = value

    spread([pg_send[r] for r in range(4)], (1, 2, 3, 4))

    def pixel_taps(f, first, rows):
        return jnp.concatenate(
            [taps[f, :, pl.ds((2 - y + first) * COLS, rows * COLS)] for y in range(3)], axis=0
        )

    def finish_out(f, cells, image, conv, cot, shifted):
        gain = wide(gains[1], 2 * COLS)
        out = image + conv
        parts = norm_parts(out, gain)
        hh = (parts[2] * parts[3]).astype(BF16)
        grad = norm_pull(parts, gain, cot)
        before = by_row(earlier, grad).astype(BF16)
        after = by_row(later, grad).astype(BF16)
        here = grad.astype(BF16)
        for n, at in enumerate(cells):
            part = slice(n * COLS, (n + 1) * COLS)
            lanes = slice(at * COLS, (at + 1) * COLS)
            head[f + 2, :, lanes] = hh[:, part]
            dout[f, :, lanes] = grad[:, part]
            dob[f, :, lanes] = here[:, part]
        shifted[0, f, 0:C] = before
        shifted[0, f, C : 3 * C // 2] = here[0 : C // 2]
        shifted[1, f, 0 : C // 2] = here[C // 2 : C]
        shifted[1, f, C // 2 : 3 * C // 2] = after

    def columns(z, first, last):
        return z[C : 2 * C] + by_row(first, z[0:C]) + by_row(last, z[2 * C : 3 * C])

    def middle_of(field, f):
        return jnp.concatenate(
            [field[f + t, :, y * COLS : (y + 2) * COLS] for y in range(3) for t in range(3)], axis=0
        )

    def edges_of(field, top, bottom, f):
        parts = []
        for y in range(3):
            for t in range(3):
                one = top[f + t] if y == 0 else field[f + t, :, (y - 1) * COLS : y * COLS]
                two = bottom[f + t] if y == 2 else field[f + t, :, (y + 2) * COLS : (y + 3) * COLS]
                parts.append(jnp.concatenate([one, two], axis=1))
        return jnp.concatenate(parts, axis=0)

    def forward_middle(f):
        conv = columns(dot(wf[...], middle_of(hin, f)), later, earlier)
        cot = dot(hwt[...], pixel_taps(f + 2, 1, 2))
        finish_out(f, (1, 2), xs[f, :, COLS : 3 * COLS], conv, cot, dsh_mid)

    for f in range(0, FR):
        forward_middle(f)

    def edge_windows(frames):
        return jnp.concatenate([edges_of(hin, hin_t, hin_b, f) for f in frames], axis=1)

    def edge_grads(half, frames):
        return jnp.concatenate([dsh_edge[half, f] for f in frames], axis=1)

    shifted = [
        jnp.concatenate([dsh_mid[half, f] for f in range(FR)], axis=1) for half in range(2)
    ]
    middle = dot_nt(
        jnp.concatenate(shifted, axis=0),
        jnp.concatenate([middle_of(hin, f) for f in range(FR)], axis=1),
    )
    mid_grads[0] = middle[0 : 3 * C // 2]
    mid_grads[1] = middle[3 * C // 2 : 3 * C]

    def head_edge_taps(f):
        return jnp.concatenate([pixel_taps(f, 0, 1), pixel_taps(f, 3, 1)], axis=1)

    def head_edges(f):
        return jnp.concatenate([head[f, :, 0:COLS], head[f, :, 3 * COLS : 4 * COLS]], axis=1)

    head_mid[...] = dot_nt(
        jnp.concatenate([pixel_taps(f, 1, 2) for f in range(8)], axis=1),
        jnp.concatenate([head[f, :, COLS : 3 * COLS] for f in range(8)], axis=1),
    )

    def hin_arrived(group):
        some = groups[group]
        shape = (some.stop - some.start, C, COLS)
        span = pl.ds(some.start, shape[0])
        whole(hin_t.at[span], hs.at[1], hr.at[0, group]).wait_recv()
        whole(hin_b.at[span], hs.at[0], hr.at[1, group]).wait_recv()

        @pl.when(me == 0)
        def _():
            hin_t[some] = jnp.zeros(shape, BF16)

        @pl.when(me == slabs - 1)
        def _():
            hin_b[some] = jnp.zeros(shape, BF16)

    for side in range(2):
        pg_copy(side).wait_recv()

    @pl.when(me == 0)
    def _():
        pg_halo[0] = jnp.zeros((32, COLS), BF16)

    @pl.when(me == slabs - 1)
    def _():
        pg_halo[1] = jnp.zeros((32, COLS), BF16)

    spread([pg_halo[0], pg_halo[1]], (0, 5))

    def forward_edges(f):
        conv = columns(dot(wf[...], edges_of(hin, hin_t, hin_b, f)), later, earlier)
        cot = dot(hwt[...], head_edge_taps(f + 2))
        image = jnp.concatenate([xs[f, :, 0:COLS], xs[f, :, 3 * COLS : 4 * COLS]], axis=1)
        finish_out(f, (0, 3), image, conv, cot, dsh_edge)

    late = range(4, FR)
    for group in range(3):
        frames = range(2 * group, 2 * group + 2)
        hin_arrived(group)
        for f in frames:
            forward_edges(f)
        for f in frames:
            for side in range(2):
                dob_copy(side, f).start()
        if group < 2:
            part = dot_nt(
                jnp.concatenate([edge_grads(0, frames), edge_grads(1, frames)], axis=0),
                edge_windows(frames),
            )
            mid_grads[0] += part[0 : 3 * C // 2]
            mid_grads[1] += part[3 * C // 2 : 3 * C]

    total = head_mid[...] + dot_nt(
        jnp.concatenate([head_edge_taps(f) for f in range(8)], axis=1),
        jnp.concatenate([head_edges(f) for f in range(8)], axis=1),
    )
    head_sum[0] = total[0 : C // 2]
    head_sum[1] = total[C // 2 : C]

    per = 64 // planes

    def where_is(tile):
        owner, k = divmod(tile, per)
        return owner, slice(k * 16, (k + 1) * 16)

    def tile_of(tile):
        row, lane = divmod(tile, 7)
        return grads[row * 16 : (row + 1) * 16, lane * COLS : (lane + 1) * COLS]

    def half_grads(half):
        grads[:, 0:K3] = mid_grads[half] + dot_nt(edge_grads(half, late), edge_windows(late))
        for n in range(3):
            rows = slice(n * (C // 2), (n + 1) * (C // 2))
            grads[rows, K3 : K3 + 32] = head_sum[half, :, n * 32 : (n + 1) * 32]

    def pair_copy():
        return remote(piece, got1, s1, r1, sibling)

    def scatter_copy(k):
        return remote(sum1.at[(xy + k) % planes], got2.at[k], s2, r2, in_plane(k))

    def z_copy():
        return remote(half3, got3, s3, r3, zpartner)

    def gather_copy(k):
        mine = full.at[core, xy]
        return remote(mine, mine, s4, r4.at[k // 4], in_plane(k))

    def pass_on(k):
        one = full.at[core, (xy + planes - k) % planes]
        return remote(one, one, s5, r5, sibling)

    half_grads(1 - core)
    for tile in range(64):
        owner, rows = where_is(tile)
        value = tile_of(tile).astype(BF16) if tile < 63 else jnp.zeros((16, COLS), BF16)
        piece[owner, rows] = value
    pair_copy().start()
    half_grads(core)

    dob[6] = jnp.zeros((C, 4 * COLS), BF16)
    dob[7] = jnp.zeros((C, 4 * COLS), BF16)
    for f in (6, 7):
        dob_t[f] = jnp.zeros((C, COLS), BF16)
        dob_b[f] = jnp.zeros((C, COLS), BF16)

    def finish_in(f, cells, conv):
        gain = wide(gains[0], 2 * COLS)
        lanes = [slice(at * COLS, (at + 1) * COLS) for at in cells]
        image = jnp.concatenate([xs[f, :, at] for at in lanes], axis=1)
        grad = norm_pull(norm_parts(image, gain), gain, conv)
        for n, at in enumerate(cells):
            value = grad[:, n * COLS : (n + 1) * COLS] + dout[f, :, lanes[n]]
            gi_ref[f, pl.ds(at, C, stride=4), :] = value

    def backward_middle(f):
        finish_in(f, (1, 2), columns(dot(wt[...], middle_of(dob, f)), earlier, later))

    def backward_edges(f):
        window = edges_of(dob, dob_t, dob_b, f)
        finish_in(f, (0, 3), columns(dot(wt[...], window), earlier, later))

    pair_copy().wait_recv()
    for tile in range(64):
        owner, rows = where_is(tile)
        value = got1[owner, rows].astype(F32)
        if tile < 63:
            value = value + tile_of(tile)
        sum1[owner, rows] = value.astype(BF16)
    for k in range(1, planes):
        scatter_copy(k).start()

    for f in range(0, FR):
        backward_middle(f)

    total = sum1[xy].astype(F32)
    whole(got2.at[pl.ds(1, planes - 1)], s2, r2).wait_recv()
    for k in range(1, planes):
        total = total + got2[k].astype(F32)
    half3[...] = total.astype(BF16)
    z_copy().start()

    whole(dob_t.at[pl.ds(0, FR)], ds.at[1], dr.at[0]).wait_recv()
    whole(dob_b.at[pl.ds(0, FR)], ds.at[0], dr.at[1]).wait_recv()

    @pl.when(me == 0)
    def _():
        dob_t[0:FR] = jnp.zeros((FR, C, COLS), BF16)

    @pl.when(me == slabs - 1)
    def _():
        dob_b[0:FR] = jnp.zeros((FR, C, COLS), BF16)

    for f in range(0, FR):
        backward_edges(f)

    z_copy().wait_recv()
    full[core, xy] = (half3[...].astype(F32) + got3[...].astype(F32)).astype(BF16)
    for k in range(1, planes):
        gather_copy(k).start()
    pass_on(0).start()
    for low in range(0, planes, 4):
        some = range(max(low, 1), min(low + 4, planes))
        whole(got2.at[pl.ds(0, len(some))], s4, r4.at[low // 4]).wait_recv()
        for k in some:
            pass_on(k).start()
    whole(full.at[1 - core], s5, r5).wait_recv()
    sums_ref[...] = full[...]

    for side in range(2):
        pg_copy(side).wait_send()
        whole(hin_t, hs.at[side], hr.at[side, 0]).wait_send()
        whole(dob_t.at[pl.ds(0, FR)], ds.at[side], dr.at[side]).wait_send()
    pair_copy().wait_send()
    whole(got2.at[pl.ds(1, planes - 1)], s2, r2).wait_send()
    z_copy().wait_send()
    whole(got2.at[pl.ds(1, planes - 1)], s4, r4.at[0]).wait_send()
    whole(full.at[core], s5, r5).wait_send()


def finish(slabs, gi_ref, sums, out_hbm, gm_hbm, gh_hbm, grads, gm, gh, outs):
    gi_out = pltpu.make_async_copy(gi_ref, out_hbm, outs.at[3])
    gi_out.start()
    planes = slabs // 4
    per = 64 // planes
    scale = (1.0 / (FR * slabs * 4 * COLS)) ** 0.5
    for half in range(2):
        for tile in range(63):
            owner, k = divmod(tile, per)
            row, lane = divmod(tile, 7)
            at = half * (3 * C // 2) + row * 16
            value = sums[half, owner, k * 16 : (k + 1) * 16].astype(F32) * scale
            grads[at : at + 16, lane * COLS : (lane + 1) * COLS] = value
    gm_out = []
    for t in range(3):
        for y in range(3):
            for x in range(3):
                at = (y * 3 + t) * C
                gm[t, y, x] = grads[x * C : (x + 1) * C, at : at + C]
        gm_out.append(pltpu.make_async_copy(gm.at[t], gm_hbm.at[t], outs.at[t]))
        gm_out[t].start()
    head = []
    for half in range(2):
        top = half * (3 * C // 2)
        parts = [
            grads[top + n * (C // 2) : top + (n + 1) * (C // 2), K3 : K3 + 32] for n in range(3)
        ]
        head.append(jnp.concatenate(parts, axis=1))
    head = jnp.concatenate(head, axis=0)
    for y in range(3):
        for x in range(3):
            for t in range(3):
                at = y * 32 + x * 9 + t * 3
                gh[2 - t, y, x] = head[at : at + 3, :]
    gh_out = pltpu.make_async_copy(gh, gh_hbm, outs.at[4])
    gh_out.start()
    for copy in [gi_out, gh_out] + gm_out:
        copy.wait()


def local(slabs, *operands):
    (x, mc, hc, gin, gout, mw, hw, ag, tab, idx, order) = operands
    planes = slabs // 4
    unit = (1024 // planes, COLS)
    plane = (planes,) + unit
    hbm = pl.BlockSpec(memory_space=pltpu.HBM)
    vmem = pl.BlockSpec(memory_space=pltpu.VMEM)
    dma = pltpu.SemaphoreType.DMA
    operands = (
        x.reshape(FR, 4 * C, COLS),
        mc.reshape(2, 4 * C, COLS),
        hc.reshape(2, 4 * C, COLS),
        gin.reshape(1, C),
        gout.reshape(1, C),
        mw,
        hw,
        ag,
        jnp.transpose(tab, (1, 2, 0)),
        idx,
        order,
    )
    gi_shape = jax.ShapeDtypeStruct((FR, 4 * C, COLS), F32)
    gi, sums = pl.pallas_call(
        functools.partial(kernel, slabs),
        out_shape=(pltpu.VMEM(gi_shape.shape, F32), pltpu.VMEM((2,) + plane, BF16)),
        in_specs=[hbm] * 11,
        out_specs=[vmem] * 2,
        scratch_shapes=[pltpu.VMEM(value.shape, value.dtype) for value in operands[:8]]
        + [pltpu.SMEM(value.shape, value.dtype) for value in operands[8:]]
        + [
            pltpu.VMEM((FR, 4 * C, COLS), F32),
            pltpu.VMEM((FR, C, 4 * COLS), F32),
            pltpu.VMEM((2, C, COLS), F32),
            pltpu.VMEM((8, C, 4 * COLS), BF16),
            pltpu.VMEM((8, C, COLS), BF16),
            pltpu.VMEM((8, C, COLS), BF16),
            pltpu.VMEM((8, C, 4 * COLS), BF16),
            pltpu.VMEM((2, 3 * C, 7 * COLS), F32),
            pltpu.VMEM((3 * C, K3), BF16),
            pltpu.VMEM((3 * C, K3), BF16),
            pltpu.VMEM((C, C), BF16),
            pltpu.VMEM((4, 32, COLS), F32),
            pltpu.VMEM((4, 32, COLS), BF16),
            pltpu.VMEM((2, 32, COLS), BF16),
            pltpu.VMEM((8, 32, 6 * COLS), BF16),
            pltpu.VMEM((FR, C, 4 * COLS), F32),
            pltpu.VMEM((8, C, 4 * COLS), BF16),
            pltpu.VMEM((8, C, COLS), BF16),
            pltpu.VMEM((8, C, COLS), BF16),
            pltpu.VMEM((2, FR, 3 * C // 2, 2 * COLS), BF16),
            pltpu.VMEM((2, FR, 3 * C // 2, 2 * COLS), BF16),
            pltpu.VMEM((2, 3 * C // 2, K3), F32),
            pltpu.VMEM((C, C), F32),
            pltpu.VMEM((2, C // 2, C), F32),
            pltpu.VMEM((3 * C // 2, 7 * COLS), F32),
            pltpu.VMEM(plane, BF16),
            pltpu.VMEM(plane, BF16),
            pltpu.VMEM(plane, BF16),
            pltpu.VMEM(plane, BF16),
            pltpu.VMEM(unit, BF16),
            pltpu.VMEM(unit, BF16),
            pltpu.VMEM((2,) + plane, BF16),
            dma((11,)),
            dma((2,)),
            dma((2, 3)),
            dma((2,)),
            dma((2,)),
            dma((2,)),
            dma((2,)),
            dma,
            dma,
            dma,
            dma,
            dma,
            dma,
            dma,
            dma(((planes + 3) // 4,)),
            dma,
            dma,
        ],
        compiler_params=pltpu.CompilerParams(
            collective_id=0, has_side_effects=True, vmem_limit_bytes=56 * 2**20
        ),
    )(*operands)
    gi, gm, gh = pl.pallas_call(
        functools.partial(finish, slabs),
        out_shape=(
            gi_shape,
            jax.ShapeDtypeStruct((3, 3, 3, C, C), F32),
            jax.ShapeDtypeStruct((3, 3, 3, 3, C), F32),
        ),
        in_specs=[vmem, vmem],
        out_specs=[hbm, hbm, hbm],
        scratch_shapes=[
            pltpu.VMEM((3 * C, 7 * COLS), F32),
            pltpu.VMEM((3, 3, 3, C, C), F32),
            pltpu.VMEM((3, 3, 3, 3, C), F32),
            dma((5,)),
        ],
        compiler_params=pltpu.CompilerParams(vmem_limit_bytes=16 * 2**20),
    )(gi, sums)
    return gi.reshape(FR, C, 4, COLS), gm, gh


def solution(mesh):
    tile = P("video", None, "slab", None)
    whole = P("video", None, None, None, None)
    placed = (tile, tile, tile, P(), P(), P(), P(), tile, P(), P("video"), P())
    return jax.shard_map(
        functools.partial(local, mesh.shape["slab"]),
        mesh=mesh,
        in_specs=placed,
        out_specs=(tile, whole, whole),
        check_vma=False,
    )
```

```python
import functools

import jax
import jax.numpy as jnp
from jax import lax
from jax.experimental import pallas as pl
from jax.experimental.pallas import tpu as pltpu
from jax.sharding import PartitionSpec as P

EPS = 1e-06
MESH = pl.DeviceIdType.MESH
F32 = jnp.float32
BF16 = jnp.bfloat16
C = 96
FR = 6
COLS = 128
K3 = 9 * C


def dot(a, b):
    return lax.dot_general(a, b, (((1,), (0,)), ((), ())), preferred_element_type=F32)


def dot_nt(a, b):
    return lax.dot_general(a, b, (((1,), (1,)), ((), ())), preferred_element_type=F32)


def lane_of(value):
    return lax.broadcasted_iota(jnp.int32, value.shape, 1)


def later(value):
    return jnp.where(lane_of(value) == 0, 0.0, pltpu.roll(value, 1, 1))


def earlier(value):
    return jnp.where(lane_of(value) == COLS - 1, 0.0, pltpu.roll(value, COLS - 1, 1))


def by_row(shift, value):
    parts = [shift(value[:, i : i + COLS]) for i in range(0, value.shape[1], COLS)]
    return jnp.concatenate(parts, axis=1)


def wide(gain, width):
    return jnp.concatenate([gain] * (width // COLS), axis=1)


def norm_parts(value, gain):
    meansq = jnp.sum(value * value, axis=0, keepdims=True) * (1.0 / C)
    root = lax.rsqrt(meansq + EPS)
    unit = value * root
    normed = unit * gain
    sig = 0.5 * jnp.tanh(0.5 * normed) + 0.5
    return root, unit, normed, sig


def norm_pull(parts, gain, cot):
    root, unit, normed, sig = parts
    inner = cot * gain * (sig * (1.0 + normed * (1.0 - sig)))
    mean = jnp.sum(inner * unit, axis=0, keepdims=True) * (1.0 / C)
    return root * (inner - unit * mean)


def tiles_of(core):
    return range(0, 16) if core == 0 else range(16, 128)


def where_is(planes, tile):
    core = 0 if tile < 16 else 1
    tiles = tiles_of(core)
    owner, k = divmod(tile - tiles[0], len(tiles) // planes)
    return owner, slice(k * 16, (k + 1) * 16)


def kernel(
    slabs,
    x_hbm,
    mc_hbm,
    hc_hbm,
    gin_hbm,
    gout_hbm,
    mw_hbm,
    hw_hbm,
    ag_hbm,
    tab_hbm,
    idx_hbm,
    ord_hbm,
    gi_ref,
    sums0_ref,
    sums1_ref,
    x_ref,
    mc_ref,
    hc_ref,
    gin_ref,
    gout_ref,
    mw_ref,
    hw_ref,
    ag_ref,
    tab_ref,
    idx_ref,
    ord_ref,
    stage,
    xs,
    gains,
    hin,
    hin_t,
    hin_b,
    head,
    wtmp,
    wf,
    wt,
    hwt,
    pg_own,
    pg_send,
    pg_halo,
    taps,
    dout,
    dob,
    dob_t,
    dob_b,
    dsh_mid,
    dsh_edge,
    mid_grads,
    head_mid,
    grads,
    piece0,
    piece1,
    got10,
    got11,
    sum10,
    sum11,
    got20,
    got21,
    half30,
    half31,
    got30,
    got31,
    full0,
    full1,
    ins,
    hs,
    hr,
    ps,
    pr,
    ds,
    dr,
    s1,
    r1,
    s2,
    r2,
    s3,
    r3,
    s4,
    r4,
    s5,
    r5,
):
    me = lax.axis_index("slab")
    core = me % 2
    place = me % 4
    zh = place // 2
    xy = me // 4
    piece = (piece0, piece1)
    got1 = (got10, got11)
    sum1 = (sum10, sum11)
    got2 = (got20, got21)
    half3 = (half30, half31)
    got3 = (got30, got31)
    full = (full0, full1)
    planes = slabs // 4
    up = (me + slabs - 1) % slabs
    down = (me + 1) % slabs
    sibling = me + 1 - 2 * core
    zpartner = me + 2 - 4 * zh

    side_len = int(planes**0.5)
    px, py = xy % side_len, xy // side_len
    offsets = [(a, b) for a in range(side_len) for b in range(side_len)]
    offsets.sort(key=lambda at: -sum(min(step, side_len - step) for step in at))
    offsets = offsets[-1:] + offsets[:-1]

    def chip_at(k):
        a, b = offsets[k]
        return (py + a) % side_len * side_len + (px + b) % side_len

    def chip_from(k):
        a, b = offsets[k]
        return (py + side_len - a) % side_len * side_len + (px + side_len - b) % side_len

    def in_plane(k):
        return chip_at(k) * 4 + place

    pairs = (
        (x_hbm, x_ref),
        (mc_hbm, mc_ref),
        (hc_hbm, hc_ref),
        (gin_hbm, gin_ref),
        (gout_hbm, gout_ref),
        (mw_hbm, mw_ref),
        (hw_hbm, hw_ref),
        (ag_hbm, ag_ref),
        (tab_hbm, tab_ref),
        (idx_hbm, idx_ref),
        (ord_hbm, ord_ref),
    )
    loads = [pltpu.make_async_copy(a, b, ins.at[n]) for n, (a, b) in enumerate(pairs)]

    def remote(src, dst, send, recv, to):
        return pltpu.make_async_remote_copy(
            src_ref=src,
            dst_ref=dst,
            send_sem=send,
            recv_sem=recv,
            device_id={"slab": to},
            device_id_type=MESH,
        )

    barrier = pltpu.get_barrier_semaphore()

    def greet(to):
        pl.semaphore_signal(barrier, inc=1, device_id={"slab": to}, device_id_type=MESH)

    loads[1].start()
    greet(up)
    greet(down)
    greet(zpartner)
    for k in range(1, planes):
        greet(in_plane(k))
    for n in (0, 3, 8, 9, 10, 7, 2, 5, 6, 4):
        loads[n].start()

    def split_rows(f, source):
        stage[f] = source.astype(F32)
        return jnp.concatenate(
            [stage[f, pl.ds(r, C, stride=4), :] for r in range(4)], axis=1
        )

    loads[1].wait()
    for j in range(2):
        hin[j] = split_rows(j, mc_ref[j]).astype(BF16)

    def pg_copy(side):
        return remote(
            pg_send.at[0 if side == 0 else 3],
            pg_halo.at[1 - side],
            ps.at[side],
            pr.at[1 - side],
            up if side == 0 else down,
        )

    groups = (slice(0, 4), slice(4, 6), slice(6, 8))

    def hin_copy(side, f):
        group = 0 if f < 4 else 1 if f < 6 else 2
        if side == 0:
            row, there = hin.at[f, :, pl.ds(0, COLS)], hin_b.at[f]
            return remote(row, there, hs.at[0], hr.at[1, group], up)
        row, there = hin.at[f, :, pl.ds(3 * COLS, COLS)], hin_t.at[f]
        return remote(row, there, hs.at[1], hr.at[0, group], down)

    def whole(ref, send, recv):
        return remote(ref, ref, send, recv, sibling)

    def dob_copy(side, f):
        if side == 0:
            row, there = dob.at[f, :, pl.ds(0, COLS)], dob_b.at[f]
            return remote(row, there, ds.at[0], dr.at[1], up)
        row, there = dob.at[f, :, pl.ds(3 * COLS, COLS)], dob_t.at[f]
        return remote(row, there, ds.at[1], dr.at[0], down)

    pl.semaphore_wait(barrier, planes + 2)
    for j in range(2):
        for side in range(2):
            hin_copy(side, j).start()

    for n in (7, 8, 9, 10):
        loads[n].wait()
    pg_own[...] = jnp.zeros_like(pg_own)
    for f in range(FR):
        picked = []
        for a in range(4):
            total = None
            for j in range(FR):
                weight = jnp.where(ord_ref[j] == f, 1.0, 0.0).astype(F32)
                term = ag_ref[j, a].astype(F32) * weight
                total = term if total is None else total + term
            picked.append(total)
        row = idx_ref[f]
        for c in range(3):
            value = picked[0] * tab_ref[c, 0, row]
            for a in range(1, 4):
                value = value + picked[a] * tab_ref[c, a, row]
            for r in range(4):
                pg_own[r, 6 + 3 * f + c : 7 + 3 * f + c, :] = value[r : r + 1, :]
    pg_send[...] = pg_own[...].astype(BF16)
    loads[0].wait()
    loads[3].wait()
    gains[0] = jnp.broadcast_to(gin_ref[...], (COLS, C)).T
    for side in range(2):
        pg_copy(side).start()

    def make_h(f):
        value = split_rows(f, x_ref[f])
        xs[f] = value
        _, _, normed, sig = norm_parts(value, wide(gains[0], 4 * COLS))
        hin[f + 2] = (normed * sig).astype(BF16)
        for side in range(2):
            hin_copy(side, f + 2).start()

    for f in range(0, FR):
        make_h(f)

    loads[4].wait()
    gains[1] = jnp.broadcast_to(gout_ref[...], (COLS, C)).T

    loads[5].wait()
    for x in range(3):
        for y in range(3):
            for t in range(3):
                at = (y * 3 + t) * C
                wtmp[0, x * C : (x + 1) * C, at : at + C] = mw_ref[t, y, x].astype(F32)
                wtmp[1, x * C : (x + 1) * C, at : at + C] = mw_ref[2 - t, 2 - y, x].astype(F32).T
    wf[...] = wtmp[0, :, 0:K3].astype(BF16)
    wt[...] = wtmp[1, :, 0:K3].astype(BF16)
    loads[6].wait()
    grads[0:C, 0:C] = jnp.zeros((C, C), F32)
    for y in range(3):
        for x in range(3):
            for t in range(3):
                at = y * 32 + x * 9 + t * 3
                grads[at : at + 3, 0:C] = hw_ref[2 - t, y, x].astype(F32)
    hwt[...] = grads[0:C, 0:C].T.astype(BF16)
    loads[2].wait()
    for j in range(2):
        head[j] = split_rows(j, hc_ref[j]).astype(BF16)

    out_row = lax.broadcasted_iota(jnp.int32, (8 * 32, C), 0)
    in_row = lax.broadcasted_iota(jnp.int32, (8 * 32, C), 1)
    frame = lax.shift_right_logical(out_row, 5)
    tap = out_row - 32 * frame
    col = jnp.where(tap >= 9, 1, 0) + jnp.where(tap >= 18, 1, 0)
    source = col * 32 + frame * 3 + (tap - 9 * col)
    chosen = jnp.where((in_row == source) & (tap < 27), 1.0, 0.0).astype(BF16)

    def spread(rows, lanes):
        rows = [value.astype(F32) for value in rows]
        stack = jnp.concatenate(
            [
                jnp.concatenate([earlier(value) for value in rows], axis=1),
                jnp.concatenate(rows, axis=1),
                jnp.concatenate([later(value) for value in rows], axis=1),
            ],
            axis=0,
        )
        result = dot(chosen, stack.astype(BF16)).astype(BF16)
        for f in range(8):
            for n, at in enumerate(lanes):
                value = result[f * 32 : (f + 1) * 32, n * COLS : (n + 1) * COLS]
                taps[f, :, at * COLS : (at + 1) * COLS] = value

    spread([pg_send[r] for r in range(4)], (1, 2, 3, 4))

    def pixel_taps(f, first, rows):
        return jnp.concatenate(
            [taps[f, :, pl.ds((2 - y + first) * COLS, rows * COLS)] for y in range(3)], axis=0
        )

    def finish_out(f, cells, image, conv, cot, shifted):
        gain = wide(gains[1], 2 * COLS)
        out = image + conv
        parts = norm_parts(out, gain)
        hh = (parts[2] * parts[3]).astype(BF16)
        grad = norm_pull(parts, gain, cot)
        before = by_row(earlier, grad).astype(BF16)
        after = by_row(later, grad).astype(BF16)
        here = grad.astype(BF16)
        for n, at in enumerate(cells):
            part = slice(n * COLS, (n + 1) * COLS)
            lanes = slice(at * COLS, (at + 1) * COLS)
            head[f + 2, :, lanes] = hh[:, part]
            dout[f, :, lanes] = grad[:, part]
            dob[f, :, lanes] = here[:, part]
        shifted[0, f, 0:C] = before
        shifted[0, f, C : 3 * C // 2] = here[0 : C // 2]
        shifted[1, f, 0 : C // 2] = here[C // 2 : C]
        shifted[1, f, C // 2 : 3 * C // 2] = after

    def columns(z, first, last):
        return z[C : 2 * C] + by_row(first, z[0:C]) + by_row(last, z[2 * C : 3 * C])

    def middle_of(field, f):
        return jnp.concatenate(
            [field[f + t, :, y * COLS : (y + 2) * COLS] for y in range(3) for t in range(3)], axis=0
        )

    def edges_of(field, top, bottom, f):
        parts = []
        for y in range(3):
            for t in range(3):
                one = top[f + t] if y == 0 else field[f + t, :, (y - 1) * COLS : y * COLS]
                two = bottom[f + t] if y == 2 else field[f + t, :, (y + 2) * COLS : (y + 3) * COLS]
                parts.append(jnp.concatenate([one, two], axis=1))
        return jnp.concatenate(parts, axis=0)

    def forward_middle(f):
        conv = columns(dot(wf[...], middle_of(hin, f)), later, earlier)
        cot = dot(hwt[...], pixel_taps(f + 2, 1, 2))
        finish_out(f, (1, 2), xs[f, :, COLS : 3 * COLS], conv, cot, dsh_mid)

    for f in range(0, FR):
        forward_middle(f)

    def edge_windows(frames):
        return jnp.concatenate([edges_of(hin, hin_t, hin_b, f) for f in frames], axis=1)

    def edge_grads(half, frames):
        return jnp.concatenate([dsh_edge[half, f] for f in frames], axis=1)

    shifted = [
        jnp.concatenate([dsh_mid[half, f] for f in range(FR)], axis=1) for half in range(2)
    ]
    middle = dot_nt(
        jnp.concatenate(shifted, axis=0),
        jnp.concatenate([middle_of(hin, f) for f in range(FR)], axis=1),
    )
    mid_grads[0] = middle[0 : 3 * C // 2]
    mid_grads[1] = middle[3 * C // 2 : 3 * C]

    def head_edge_taps(f):
        return jnp.concatenate([pixel_taps(f, 0, 1), pixel_taps(f, 3, 1)], axis=1)

    def head_edges(f):
        return jnp.concatenate([head[f, :, 0:COLS], head[f, :, 3 * COLS : 4 * COLS]], axis=1)

    head_mid[...] = dot_nt(
        jnp.concatenate([pixel_taps(f, 1, 2) for f in range(8)], axis=1),
        jnp.concatenate([head[f, :, COLS : 3 * COLS] for f in range(8)], axis=1),
    )

    def hin_arrived(group):
        some = groups[group]
        shape = (some.stop - some.start, C, COLS)
        span = pl.ds(some.start, shape[0])
        whole(hin_t.at[span], hs.at[1], hr.at[0, group]).wait_recv()
        whole(hin_b.at[span], hs.at[0], hr.at[1, group]).wait_recv()

        @pl.when(me == 0)
        def _():
            hin_t[some] = jnp.zeros(shape, BF16)

        @pl.when(me == slabs - 1)
        def _():
            hin_b[some] = jnp.zeros(shape, BF16)

    for side in range(2):
        pg_copy(side).wait_recv()

    @pl.when(me == 0)
    def _():
        pg_halo[0] = jnp.zeros((32, COLS), BF16)

    @pl.when(me == slabs - 1)
    def _():
        pg_halo[1] = jnp.zeros((32, COLS), BF16)

    spread([pg_halo[0], pg_halo[1]], (0, 5))

    def forward_edges(f):
        conv = columns(dot(wf[...], edges_of(hin, hin_t, hin_b, f)), later, earlier)
        cot = dot(hwt[...], head_edge_taps(f + 2))
        image = jnp.concatenate([xs[f, :, 0:COLS], xs[f, :, 3 * COLS : 4 * COLS]], axis=1)
        finish_out(f, (0, 3), image, conv, cot, dsh_edge)

    late = range(4, FR)
    for group in range(3):
        frames = range(2 * group, 2 * group + 2)
        hin_arrived(group)
        for f in frames:
            forward_edges(f)
        for f in frames:
            for side in range(2):
                dob_copy(side, f).start()
        if group < 2:
            part = dot_nt(
                jnp.concatenate([edge_grads(0, frames), edge_grads(1, frames)], axis=0),
                edge_windows(frames),
            )
            mid_grads[0] += part[0 : 3 * C // 2]
            mid_grads[1] += part[3 * C // 2 : 3 * C]

    total = head_mid[...] + dot_nt(
        jnp.concatenate([head_edge_taps(f) for f in range(8)], axis=1),
        jnp.concatenate([head_edges(f) for f in range(8)], axis=1),
    )
    part = dot_nt(
        jnp.concatenate([edge_grads(0, late), edge_grads(1, late)], axis=0), edge_windows(late)
    )
    for half in range(2):
        rows = slice(half * (3 * C // 2), (half + 1) * (3 * C // 2))
        grads[rows, 0:K3] = mid_grads[half] + part[rows]
    for n in range(3):
        grads[n * C : (n + 1) * C, K3 : K3 + 32] = total[:, n * 32 : (n + 1) * 32]

    def tile_of(tile):
        row, lane = divmod(tile, 7)
        return grads[row * 16 : (row + 1) * 16, lane * COLS : (lane + 1) * COLS]

    def pair_copy(c):
        return remote(piece[1 - c], got1[1 - c], s1, r1, sibling)

    def scatter_copy(c, k):
        part = sum1[c].at[chip_at(k)]
        return remote(part, got2[c].at[k], s2, r2, in_plane(k))

    def z_copy(c):
        return remote(half3[c], got3[c], s3, r3, zpartner)

    def gather_copy(c, k):
        mine = full[c].at[xy]
        return remote(mine, mine, s4, r4.at[k // 4], in_plane(k))

    def pass_on(c, k):
        one = full[c].at[chip_from(k)]
        return remote(one, one, s5, r5, sibling)

    def others(c):
        return got2[c].at[pl.ds(1, planes - 1)]

    def on_core(stage):
        for c in range(2):
            pl.when(core == c)(functools.partial(stage, c))

    def start_pair(c):
        for tile in tiles_of(1 - c):
            owner, rows = where_is(planes, tile)
            value = tile_of(tile).astype(BF16) if tile < 126 else jnp.zeros((16, COLS), BF16)
            piece[1 - c][owner, rows] = value
        pair_copy(c).start()

    def start_scatter(c):
        whole(got1[c], s1, r1).wait_recv()
        for tile in tiles_of(c):
            owner, rows = where_is(planes, tile)
            value = got1[c][owner, rows].astype(F32)
            if tile < 126:
                value = value + tile_of(tile)
            sum1[c][owner, rows] = value.astype(BF16)
        for k in range(1, planes):
            scatter_copy(c, k).start()

    def start_z(c):
        whole(others(c), s2, r2).wait_recv()
        total = sum1[c][xy].astype(F32)
        for k in range(1, planes):
            total = total + got2[c][k].astype(F32)
        half3[c][...] = total.astype(BF16)
        z_copy(c).start()

    def gather(c):
        z_copy(c).wait_recv()
        full[c][xy] = (half3[c][...].astype(F32) + got3[c][...].astype(F32)).astype(BF16)
        for k in range(1, planes):
            gather_copy(c, k).start()
        pass_on(c, 0).start()
        for low in range(0, planes, 4):
            some = range(max(low, 1), min(low + 4, planes))
            whole(got2[c].at[pl.ds(0, len(some))], s4, r4.at[low // 4]).wait_recv()
            for k in some:
                pass_on(c, k).start()
        whole(full[1 - c], s5, r5).wait_recv()

    def sums_left(c):
        pair_copy(c).wait_send()
        whole(others(c), s2, r2).wait_send()
        z_copy(c).wait_send()
        whole(others(c), s4, r4.at[0]).wait_send()
        whole(full[c], s5, r5).wait_send()

    on_core(start_pair)

    dob[6] = jnp.zeros((C, 4 * COLS), BF16)
    dob[7] = jnp.zeros((C, 4 * COLS), BF16)
    for f in (6, 7):
        dob_t[f] = jnp.zeros((C, COLS), BF16)
        dob_b[f] = jnp.zeros((C, COLS), BF16)

    def finish_in(f, cells, conv):
        gain = wide(gains[0], 2 * COLS)
        lanes = [slice(at * COLS, (at + 1) * COLS) for at in cells]
        image = jnp.concatenate([xs[f, :, at] for at in lanes], axis=1)
        grad = norm_pull(norm_parts(image, gain), gain, conv)
        for n, at in enumerate(cells):
            value = grad[:, n * COLS : (n + 1) * COLS] + dout[f, :, lanes[n]]
            gi_ref[f, pl.ds(at, C, stride=4), :] = value

    def backward_middle(f):
        finish_in(f, (1, 2), columns(dot(wt[...], middle_of(dob, f)), earlier, later))

    def backward_edges(f):
        window = edges_of(dob, dob_t, dob_b, f)
        finish_in(f, (0, 3), columns(dot(wt[...], window), earlier, later))

    on_core(start_scatter)

    for f in range(0, FR):
        backward_middle(f)

    on_core(start_z)

    whole(dob_t.at[pl.ds(0, FR)], ds.at[1], dr.at[0]).wait_recv()
    whole(dob_b.at[pl.ds(0, FR)], ds.at[0], dr.at[1]).wait_recv()

    @pl.when(me == 0)
    def _():
        dob_t[0:FR] = jnp.zeros((FR, C, COLS), BF16)

    @pl.when(me == slabs - 1)
    def _():
        dob_b[0:FR] = jnp.zeros((FR, C, COLS), BF16)

    for f in range(0, FR):
        backward_edges(f)

    on_core(gather)
    sums0_ref[...] = full[0][...]
    sums1_ref[...] = full[1][...]

    for side in range(2):
        pg_copy(side).wait_send()
        whole(hin_t, hs.at[side], hr.at[side, 0]).wait_send()
        whole(dob_t.at[pl.ds(0, FR)], ds.at[side], dr.at[side]).wait_send()
    on_core(sums_left)


def finish(slabs, gi_ref, sums0, sums1, out_hbm, gm_hbm, gh_hbm, grads, gm, gh, outs):
    gi_out = pltpu.make_async_copy(gi_ref, out_hbm, outs.at[3])
    gi_out.start()
    planes = slabs // 4
    scale = (1.0 / (FR * slabs * 4 * COLS)) ** 0.5
    for c, sums in enumerate((sums0, sums1)):
        for tile in tiles_of(c):
            if tile < 126:
                owner, rows = where_is(planes, tile)
                row, lane = divmod(tile, 7)
                value = sums[owner, rows].astype(F32) * scale
                grads[row * 16 : (row + 1) * 16, lane * COLS : (lane + 1) * COLS] = value
    gm_out = []
    for t in range(3):
        for y in range(3):
            for x in range(3):
                at = (y * 3 + t) * C
                gm[t, y, x] = grads[x * C : (x + 1) * C, at : at + C]
        gm_out.append(pltpu.make_async_copy(gm.at[t], gm_hbm.at[t], outs.at[t]))
        gm_out[t].start()
    head = jnp.concatenate([grads[n * C : (n + 1) * C, K3 : K3 + 32] for n in range(3)], axis=1)
    for y in range(3):
        for x in range(3):
            for t in range(3):
                at = y * 32 + x * 9 + t * 3
                gh[2 - t, y, x] = head[at : at + 3, :]
    gh_out = pltpu.make_async_copy(gh, gh_hbm, outs.at[4])
    gh_out.start()
    for copy in [gi_out, gh_out] + gm_out:
        copy.wait()


def local(slabs, *operands):
    (x, mc, hc, gin, gout, mw, hw, ag, tab, idx, order) = operands
    planes = slabs // 4
    share = [(planes, 16 * len(tiles_of(c)) // planes, COLS) for c in range(2)]
    hbm = pl.BlockSpec(memory_space=pltpu.HBM)
    vmem = pl.BlockSpec(memory_space=pltpu.VMEM)
    dma = pltpu.SemaphoreType.DMA
    operands = (
        x.reshape(FR, 4 * C, COLS),
        mc.reshape(2, 4 * C, COLS),
        hc.reshape(2, 4 * C, COLS),
        gin.reshape(1, C),
        gout.reshape(1, C),
        mw,
        hw,
        ag,
        jnp.transpose(tab, (1, 2, 0)),
        idx,
        order,
    )
    gi_shape = jax.ShapeDtypeStruct((FR, 4 * C, COLS), F32)
    gi, sums0, sums1 = pl.pallas_call(
        functools.partial(kernel, slabs),
        out_shape=(pltpu.VMEM(gi_shape.shape, F32),) + tuple(
            pltpu.VMEM(plane, BF16) for plane in share
        ),
        in_specs=[hbm] * 11,
        out_specs=[vmem] * 3,
        scratch_shapes=[pltpu.VMEM(value.shape, value.dtype) for value in operands[:8]]
        + [pltpu.SMEM(value.shape, value.dtype) for value in operands[8:]]
        + [
            pltpu.VMEM((FR, 4 * C, COLS), F32),
            pltpu.VMEM((FR, C, 4 * COLS), F32),
            pltpu.VMEM((2, C, COLS), F32),
            pltpu.VMEM((8, C, 4 * COLS), BF16),
            pltpu.VMEM((8, C, COLS), BF16),
            pltpu.VMEM((8, C, COLS), BF16),
            pltpu.VMEM((8, C, 4 * COLS), BF16),
            pltpu.VMEM((2, 3 * C, 7 * COLS), F32),
            pltpu.VMEM((3 * C, K3), BF16),
            pltpu.VMEM((3 * C, K3), BF16),
            pltpu.VMEM((C, C), BF16),
            pltpu.VMEM((4, 32, COLS), F32),
            pltpu.VMEM((4, 32, COLS), BF16),
            pltpu.VMEM((2, 32, COLS), BF16),
            pltpu.VMEM((8, 32, 6 * COLS), BF16),
            pltpu.VMEM((FR, C, 4 * COLS), F32),
            pltpu.VMEM((8, C, 4 * COLS), BF16),
            pltpu.VMEM((8, C, COLS), BF16),
            pltpu.VMEM((8, C, COLS), BF16),
            pltpu.VMEM((2, FR, 3 * C // 2, 2 * COLS), BF16),
            pltpu.VMEM((2, FR, 3 * C // 2, 2 * COLS), BF16),
            pltpu.VMEM((2, 3 * C // 2, K3), F32),
            pltpu.VMEM((C, C), F32),
            pltpu.VMEM((3 * C, 7 * COLS), F32),
            *[pltpu.VMEM(plane, BF16) for _ in range(4) for plane in share],
            *[pltpu.VMEM(plane[1:], BF16) for _ in range(2) for plane in share],
            *[pltpu.VMEM(plane, BF16) for plane in share],
            dma((11,)),
            dma((2,)),
            dma((2, 3)),
            dma((2,)),
            dma((2,)),
            dma((2,)),
            dma((2,)),
            dma,
            dma,
            dma,
            dma,
            dma,
            dma,
            dma,
            dma(((planes + 3) // 4,)),
            dma,
            dma,
        ],
        compiler_params=pltpu.CompilerParams(
            collective_id=0, has_side_effects=True, vmem_limit_bytes=56 * 2**20
        ),
    )(*operands)
    gi, gm, gh = pl.pallas_call(
        functools.partial(finish, slabs),
        out_shape=(
            gi_shape,
            jax.ShapeDtypeStruct((3, 3, 3, C, C), F32),
            jax.ShapeDtypeStruct((3, 3, 3, 3, C), F32),
        ),
        in_specs=[vmem] * 3,
        out_specs=[hbm, hbm, hbm],
        scratch_shapes=[
            pltpu.VMEM((3 * C, 7 * COLS), F32),
            pltpu.VMEM((3, 3, 3, C, C), F32),
            pltpu.VMEM((3, 3, 3, 3, C), F32),
            dma((5,)),
        ],
        compiler_params=pltpu.CompilerParams(vmem_limit_bytes=16 * 2**20),
    )(gi, sums0, sums1)
    return gi.reshape(FR, C, 4, COLS), gm, gh


def solution(mesh):
    tile = P("video", None, "slab", None)
    whole = P("video", None, None, None, None)
    placed = (tile, tile, tile, P(), P(), P(), P(), tile, P(), P("video"), P())
    return jax.shard_map(
        functools.partial(local, mesh.shape["slab"]),
        mesh=mesh,
        in_specs=placed,
        out_specs=(tile, whole, whole),
        check_vma=False,
    )
```

```python
import functools

import jax
import jax.numpy as jnp
from jax import lax
from jax.experimental import pallas as pl
from jax.experimental.pallas import tpu as pltpu
from jax.sharding import PartitionSpec as P

EPS = 1e-06
MESH = pl.DeviceIdType.MESH
F32 = jnp.float32
BF16 = jnp.bfloat16
C = 96
FR = 6
COLS = 128
K3 = 9 * C


def dot(a, b):
    return lax.dot_general(a, b, (((1,), (0,)), ((), ())), preferred_element_type=F32)


def dot_nt(a, b):
    return lax.dot_general(a, b, (((1,), (1,)), ((), ())), preferred_element_type=F32)


def lane_of(value):
    return lax.broadcasted_iota(jnp.int32, value.shape, 1)


def later(value):
    return jnp.where(lane_of(value) == 0, 0.0, pltpu.roll(value, 1, 1))


def earlier(value):
    return jnp.where(lane_of(value) == COLS - 1, 0.0, pltpu.roll(value, COLS - 1, 1))


def by_row(shift, value):
    parts = [shift(value[:, i : i + COLS]) for i in range(0, value.shape[1], COLS)]
    return jnp.concatenate(parts, axis=1)


def wide(gain, width):
    return jnp.concatenate([gain] * (width // COLS), axis=1)


def norm_parts(value, gain):
    meansq = jnp.sum(value * value, axis=0, keepdims=True) * (1.0 / C)
    root = lax.rsqrt(meansq + EPS)
    unit = value * root
    normed = unit * gain
    sig = 0.5 * jnp.tanh(0.5 * normed) + 0.5
    return root, unit, normed, sig


def norm_pull(parts, gain, cot):
    root, unit, normed, sig = parts
    inner = cot * gain * (sig * (1.0 + normed * (1.0 - sig)))
    mean = jnp.sum(inner * unit, axis=0, keepdims=True) * (1.0 / C)
    return root * (inner - unit * mean)


def tiles_of(core):
    return range(0, 16) if core == 0 else range(16, 128)


def where_is(planes, tile):
    core = 0 if tile < 16 else 1
    tiles = tiles_of(core)
    owner, k = divmod(tile - tiles[0], len(tiles) // planes)
    return owner, slice(k * 16, (k + 1) * 16)


def kernel(
    slabs,
    x_hbm,
    mc_hbm,
    hc_hbm,
    gin_hbm,
    gout_hbm,
    mw_hbm,
    hw_hbm,
    ag_hbm,
    tab_hbm,
    idx_hbm,
    ord_hbm,
    gi_ref,
    sums0_ref,
    sums1_ref,
    x_ref,
    mc_ref,
    hc_ref,
    gin_ref,
    gout_ref,
    mw_ref,
    hw_ref,
    ag_ref,
    tab_ref,
    idx_ref,
    ord_ref,
    stage,
    xs,
    gains,
    hin,
    hin_t,
    hin_b,
    head,
    wtmp,
    wf,
    wt,
    hwt,
    pg_own,
    pg_send,
    pg_halo,
    taps,
    dout,
    dob,
    dob_t,
    dob_b,
    dsh_mid,
    dsh_edge,
    mid_grads,
    head_mid,
    grads,
    piece0,
    piece1,
    got10,
    got11,
    sum10,
    sum11,
    got20,
    got21,
    half30,
    half31,
    got30,
    got31,
    full0,
    full1,
    ins,
    hs,
    hr,
    ps,
    pr,
    ds,
    dr,
    s1,
    r1,
    s2,
    r2,
    s3,
    r3,
    s4,
    r4,
    s5,
    r5,
):
    me = lax.axis_index("slab")
    core = me % 2
    place = me % 4
    zh = place // 2
    xy = me // 4
    piece = (piece0, piece1)
    got1 = (got10, got11)
    sum1 = (sum10, sum11)
    got2 = (got20, got21)
    half3 = (half30, half31)
    got3 = (got30, got31)
    full = (full0, full1)
    planes = slabs // 4
    up = (me + slabs - 1) % slabs
    down = (me + 1) % slabs
    sibling = me + 1 - 2 * core
    zpartner = me + 2 - 4 * zh

    side_len = int(planes**0.5)
    px, py = xy % side_len, xy // side_len
    offsets = [(a, b) for a in range(side_len) for b in range(side_len)]
    offsets.sort(key=lambda at: -sum(min(step, side_len - step) for step in at))
    offsets = offsets[-1:] + offsets[:-1]

    def chip_at(k):
        a, b = offsets[k]
        return (py + a) % side_len * side_len + (px + b) % side_len

    def chip_from(k):
        a, b = offsets[k]
        return (py + side_len - a) % side_len * side_len + (px + side_len - b) % side_len

    def in_plane(k):
        return chip_at(k) * 4 + place

    pairs = (
        (x_hbm, x_ref),
        (mc_hbm, mc_ref),
        (hc_hbm, hc_ref),
        (gin_hbm, gin_ref),
        (gout_hbm, gout_ref),
        (mw_hbm, mw_ref),
        (hw_hbm, hw_ref),
        (ag_hbm, ag_ref),
        (tab_hbm, tab_ref),
        (idx_hbm, idx_ref),
        (ord_hbm, ord_ref),
    )
    loads = [pltpu.make_async_copy(a, b, ins.at[n]) for n, (a, b) in enumerate(pairs)]

    def remote(src, dst, send, recv, to):
        return pltpu.make_async_remote_copy(
            src_ref=src,
            dst_ref=dst,
            send_sem=send,
            recv_sem=recv,
            device_id={"slab": to},
            device_id_type=MESH,
        )

    barrier = pltpu.get_barrier_semaphore()

    def greet(to):
        pl.semaphore_signal(barrier, inc=1, device_id={"slab": to}, device_id_type=MESH)

    loads[1].start()
    greet(up)
    greet(down)
    greet(zpartner)
    for k in range(1, planes):
        greet(in_plane(k))
    for n in (0, 3, 8, 9, 10, 7, 2, 5, 6, 4):
        loads[n].start()

    def split_rows(f, source):
        stage[f] = source.astype(F32)
        return jnp.concatenate(
            [stage[f, pl.ds(r, C, stride=4), :] for r in range(4)], axis=1
        )

    loads[1].wait()
    for j in range(2):
        hin[j] = split_rows(j, mc_ref[j]).astype(BF16)

    def pg_copy(side):
        return remote(
            pg_send.at[0 if side == 0 else 3],
            pg_halo.at[1 - side],
            ps.at[side],
            pr.at[1 - side],
            up if side == 0 else down,
        )

    groups = (slice(0, 4), slice(4, 6), slice(6, 8))

    def hin_copy(side, f):
        group = 0 if f < 4 else 1 if f < 6 else 2
        if side == 0:
            row, there = hin.at[f, :, pl.ds(0, COLS)], hin_b.at[f]
            return remote(row, there, hs.at[0], hr.at[1, group], up)
        row, there = hin.at[f, :, pl.ds(3 * COLS, COLS)], hin_t.at[f]
        return remote(row, there, hs.at[1], hr.at[0, group], down)

    def whole(ref, send, recv):
        return remote(ref, ref, send, recv, sibling)

    def dob_copy(side, f):
        if side == 0:
            row, there = dob.at[f, :, pl.ds(0, COLS)], dob_b.at[f]
            return remote(row, there, ds.at[0], dr.at[1], up)
        row, there = dob.at[f, :, pl.ds(3 * COLS, COLS)], dob_t.at[f]
        return remote(row, there, ds.at[1], dr.at[0], down)

    pl.semaphore_wait(barrier, planes + 2)
    for j in range(2):
        for side in range(2):
            hin_copy(side, j).start()

    for n in (7, 8, 9, 10):
        loads[n].wait()
    pg_own[...] = jnp.zeros_like(pg_own)
    for f in range(FR):
        picked = []
        for a in range(4):
            total = None
            for j in range(FR):
                weight = jnp.where(ord_ref[j] == f, 1.0, 0.0).astype(F32)
                term = ag_ref[j, a].astype(F32) * weight
                total = term if total is None else total + term
            picked.append(total)
        row = idx_ref[f]
        for c in range(3):
            value = picked[0] * tab_ref[c, 0, row]
            for a in range(1, 4):
                value = value + picked[a] * tab_ref[c, a, row]
            for r in range(4):
                pg_own[r, 6 + 3 * f + c : 7 + 3 * f + c, :] = value[r : r + 1, :]
    pg_send[...] = pg_own[...].astype(BF16)
    loads[0].wait()
    loads[3].wait()
    gains[0] = jnp.broadcast_to(gin_ref[...], (COLS, C)).T
    for side in range(2):
        pg_copy(side).start()

    def make_h(f):
        value = split_rows(f, x_ref[f])
        xs[f] = value
        _, _, normed, sig = norm_parts(value, wide(gains[0], 4 * COLS))
        hin[f + 2] = (normed * sig).astype(BF16)
        for side in range(2):
            hin_copy(side, f + 2).start()

    for f in range(0, FR):
        make_h(f)

    loads[4].wait()
    gains[1] = jnp.broadcast_to(gout_ref[...], (COLS, C)).T

    loads[5].wait()
    for x in range(3):
        for y in range(3):
            for t in range(3):
                at = (y * 3 + t) * C
                wtmp[0, x * C : (x + 1) * C, at : at + C] = mw_ref[t, y, x].astype(F32)
                wtmp[1, x * C : (x + 1) * C, at : at + C] = mw_ref[2 - t, 2 - y, x].astype(F32).T
    wf[...] = wtmp[0, :, 0:K3].astype(BF16)
    wt[...] = wtmp[1, :, 0:K3].astype(BF16)
    loads[6].wait()
    grads[0:C, 0:C] = jnp.zeros((C, C), F32)
    for y in range(3):
        for x in range(3):
            for t in range(3):
                at = y * 32 + x * 9 + t * 3
                grads[at : at + 3, 0:C] = hw_ref[2 - t, y, x].astype(F32)
    hwt[...] = grads[0:C, 0:C].T.astype(BF16)
    loads[2].wait()
    for j in range(2):
        head[j] = split_rows(j, hc_ref[j]).astype(BF16)

    out_row = lax.broadcasted_iota(jnp.int32, (8 * 32, C), 0)
    in_row = lax.broadcasted_iota(jnp.int32, (8 * 32, C), 1)
    frame = lax.shift_right_logical(out_row, 5)
    tap = out_row - 32 * frame
    col = jnp.where(tap >= 9, 1, 0) + jnp.where(tap >= 18, 1, 0)
    source = col * 32 + frame * 3 + (tap - 9 * col)
    chosen = jnp.where((in_row == source) & (tap < 27), 1.0, 0.0).astype(BF16)

    def spread(rows, lanes):
        rows = [value.astype(F32) for value in rows]
        stack = jnp.concatenate(
            [
                jnp.concatenate([earlier(value) for value in rows], axis=1),
                jnp.concatenate(rows, axis=1),
                jnp.concatenate([later(value) for value in rows], axis=1),
            ],
            axis=0,
        )
        result = dot(chosen, stack.astype(BF16)).astype(BF16)
        for f in range(8):
            for n, at in enumerate(lanes):
                value = result[f * 32 : (f + 1) * 32, n * COLS : (n + 1) * COLS]
                taps[f, :, at * COLS : (at + 1) * COLS] = value

    spread([pg_send[r] for r in range(4)], (1, 2, 3, 4))

    def pixel_taps(f, first, rows):
        return jnp.concatenate(
            [taps[f, :, pl.ds((2 - y + first) * COLS, rows * COLS)] for y in range(3)], axis=0
        )

    def finish_out(f, cells, image, conv, cot, shifted):
        gain = wide(gains[1], 2 * COLS)
        out = image + conv
        parts = norm_parts(out, gain)
        hh = (parts[2] * parts[3]).astype(BF16)
        grad = norm_pull(parts, gain, cot)
        before = by_row(earlier, grad).astype(BF16)
        after = by_row(later, grad).astype(BF16)
        here = grad.astype(BF16)
        for n, at in enumerate(cells):
            part = slice(n * COLS, (n + 1) * COLS)
            lanes = slice(at * COLS, (at + 1) * COLS)
            head[f + 2, :, lanes] = hh[:, part]
            dout[f, :, lanes] = grad[:, part]
            dob[f, :, lanes] = here[:, part]
        shifted[0, f, 0:C] = before
        shifted[0, f, C : 3 * C // 2] = here[0 : C // 2]
        shifted[1, f, 0 : C // 2] = here[C // 2 : C]
        shifted[1, f, C // 2 : 3 * C // 2] = after

    def columns(z, first, last):
        return z[C : 2 * C] + by_row(first, z[0:C]) + by_row(last, z[2 * C : 3 * C])

    def middle_of(field, f):
        return jnp.concatenate(
            [field[f + t, :, y * COLS : (y + 2) * COLS] for y in range(3) for t in range(3)], axis=0
        )

    def edges_of(field, top, bottom, f):
        parts = []
        for y in range(3):
            for t in range(3):
                one = top[f + t] if y == 0 else field[f + t, :, (y - 1) * COLS : y * COLS]
                two = bottom[f + t] if y == 2 else field[f + t, :, (y + 2) * COLS : (y + 3) * COLS]
                parts.append(jnp.concatenate([one, two], axis=1))
        return jnp.concatenate(parts, axis=0)

    def forward_middle(f):
        conv = columns(dot(wf[...], middle_of(hin, f)), later, earlier)
        cot = dot(hwt[...], pixel_taps(f + 2, 1, 2))
        finish_out(f, (1, 2), xs[f, :, COLS : 3 * COLS], conv, cot, dsh_mid)

    for f in range(0, FR):
        forward_middle(f)

    def edge_windows(frames):
        return jnp.concatenate([edges_of(hin, hin_t, hin_b, f) for f in frames], axis=1)

    def edge_grads(half, frames):
        return jnp.concatenate([dsh_edge[half, f] for f in frames], axis=1)

    shifted = [
        jnp.concatenate([dsh_mid[half, f] for f in range(FR)], axis=1) for half in range(2)
    ]
    middle = dot_nt(
        jnp.concatenate(shifted, axis=0),
        jnp.concatenate([middle_of(hin, f) for f in range(FR)], axis=1),
    )
    mid_grads[0] = middle[0 : 3 * C // 2]
    mid_grads[1] = middle[3 * C // 2 : 3 * C]

    def head_edge_taps(f):
        return jnp.concatenate([pixel_taps(f, 0, 1), pixel_taps(f, 3, 1)], axis=1)

    def head_edges(f):
        return jnp.concatenate([head[f, :, 0:COLS], head[f, :, 3 * COLS : 4 * COLS]], axis=1)

    head_mid[...] = dot_nt(
        jnp.concatenate([pixel_taps(f, 1, 2) for f in range(8)], axis=1),
        jnp.concatenate([head[f, :, COLS : 3 * COLS] for f in range(8)], axis=1),
    )

    def hin_arrived(group):
        some = groups[group]
        shape = (some.stop - some.start, C, COLS)
        span = pl.ds(some.start, shape[0])
        whole(hin_t.at[span], hs.at[1], hr.at[0, group]).wait_recv()
        whole(hin_b.at[span], hs.at[0], hr.at[1, group]).wait_recv()

        @pl.when(me == 0)
        def _():
            hin_t[some] = jnp.zeros(shape, BF16)

        @pl.when(me == slabs - 1)
        def _():
            hin_b[some] = jnp.zeros(shape, BF16)

    for side in range(2):
        pg_copy(side).wait_recv()

    @pl.when(me == 0)
    def _():
        pg_halo[0] = jnp.zeros((32, COLS), BF16)

    @pl.when(me == slabs - 1)
    def _():
        pg_halo[1] = jnp.zeros((32, COLS), BF16)

    spread([pg_halo[0], pg_halo[1]], (0, 5))

    def forward_edges(f):
        conv = columns(dot(wf[...], edges_of(hin, hin_t, hin_b, f)), later, earlier)
        cot = dot(hwt[...], head_edge_taps(f + 2))
        image = jnp.concatenate([xs[f, :, 0:COLS], xs[f, :, 3 * COLS : 4 * COLS]], axis=1)
        finish_out(f, (0, 3), image, conv, cot, dsh_edge)

    def head_part(frames):
        return dot_nt(
            jnp.concatenate([head_edge_taps(f) for f in frames], axis=1),
            jnp.concatenate([head_edges(f) for f in frames], axis=1),
        )

    late = range(4, FR)
    for group in range(3):
        frames = range(2 * group, 2 * group + 2)
        hin_arrived(group)
        for f in frames:
            forward_edges(f)
        for f in frames:
            for side in range(2):
                dob_copy(side, f).start()
        if group < 2:
            part = dot_nt(
                jnp.concatenate([edge_grads(0, frames), edge_grads(1, frames)], axis=0),
                edge_windows(frames),
            )
            mid_grads[0] += part[0 : 3 * C // 2]
            mid_grads[1] += part[3 * C // 2 : 3 * C]
        if group == 1:
            head_mid[...] += head_part(range(6))

    total = head_mid[...] + head_part(range(6, 8))
    part = dot_nt(
        jnp.concatenate([edge_grads(0, late), edge_grads(1, late)], axis=0), edge_windows(late)
    )
    for half in range(2):
        rows = slice(half * (3 * C // 2), (half + 1) * (3 * C // 2))
        grads[rows, 0:K3] = mid_grads[half] + part[rows]
    for n in range(3):
        grads[n * C : (n + 1) * C, K3 : K3 + 32] = total[:, n * 32 : (n + 1) * 32]

    def tile_of(tile):
        row, lane = divmod(tile, 7)
        return grads[row * 16 : (row + 1) * 16, lane * COLS : (lane + 1) * COLS]

    def pair_copy(c):
        return remote(piece[1 - c], got1[1 - c], s1, r1, sibling)

    def parts_of(c):
        rows = 16 * len(tiles_of(c)) // planes
        cut = (rows // 16 + 1) // 2 * 16
        return [span for span in (pl.ds(0, cut), pl.ds(cut, rows - cut)) if span.size]

    def scatter_copy(c, k, n):
        span = parts_of(c)[n]
        there = got2[c].at[k, span]
        return remote(sum1[c].at[chip_at(k), span], there, s2.at[n], r2.at[n], in_plane(k))

    def z_copy(c, n):
        span = parts_of(c)[n]
        return remote(half3[c].at[span], got3[c].at[span], s3.at[n], r3.at[n], zpartner)

    def gather_copy(c, k, n):
        mine = full[c].at[xy, parts_of(c)[n]]
        return remote(mine, mine, s4.at[n], r4.at[n, k // 4], in_plane(k))

    def pass_on(c, k, n):
        one = full[c].at[chip_from(k), parts_of(c)[n]]
        return remote(one, one, s5, r5, sibling)

    def others(c, n, low=1, high=planes):
        return got2[c].at[pl.ds(low, high - low), parts_of(c)[n]]

    def on_core(stage):
        for c in range(2):
            pl.when(core == c)(functools.partial(stage, c))

    def start_pair(c):
        for tile in tiles_of(1 - c):
            owner, rows = where_is(planes, tile)
            value = tile_of(tile).astype(BF16) if tile < 126 else jnp.zeros((16, COLS), BF16)
            piece[1 - c][owner, rows] = value
        pair_copy(c).start()

    def start_scatter(c):
        whole(got1[c], s1, r1).wait_recv()
        for tile in tiles_of(c):
            owner, rows = where_is(planes, tile)
            value = got1[c][owner, rows].astype(F32)
            if tile < 126:
                value = value + tile_of(tile)
            sum1[c][owner, rows] = value.astype(BF16)
        for n in range(len(parts_of(c))):
            for k in range(1, planes):
                scatter_copy(c, k, n).start()

    def start_z(c):
        for n, span in enumerate(parts_of(c)):
            whole(others(c, n), s2.at[n], r2.at[n]).wait_recv()
            total = sum1[c][xy, span].astype(F32)
            for k in range(1, planes):
                total = total + got2[c][k, span].astype(F32)
            half3[c][span] = total.astype(BF16)
            z_copy(c, n).start()

    def gather(c):
        for n, span in enumerate(parts_of(c)):
            z_copy(c, n).wait_recv()
            both = half3[c][span].astype(F32) + got3[c][span].astype(F32)
            full[c][xy, span] = both.astype(BF16)
            for k in range(1, planes):
                gather_copy(c, k, n).start()
            pass_on(c, 0, n).start()
        for n in range(len(parts_of(c))):
            for low in range(0, planes, 4):
                some = range(max(low, 1), min(low + 4, planes))
                arrived = others(c, n, 0, len(some))
                whole(arrived, s4.at[n], r4.at[n, low // 4]).wait_recv()
                for k in some:
                    pass_on(c, k, n).start()
        whole(full[1 - c], s5, r5).wait_recv()

    def sums_left(c):
        pair_copy(c).wait_send()
        for n in range(len(parts_of(c))):
            whole(others(c, n), s2.at[n], r2.at[n]).wait_send()
            z_copy(c, n).wait_send()
            whole(others(c, n), s4.at[n], r4.at[n, 0]).wait_send()
        whole(full[c], s5, r5).wait_send()

    on_core(start_pair)

    dob[6] = jnp.zeros((C, 4 * COLS), BF16)
    dob[7] = jnp.zeros((C, 4 * COLS), BF16)
    for f in (6, 7):
        dob_t[f] = jnp.zeros((C, COLS), BF16)
        dob_b[f] = jnp.zeros((C, COLS), BF16)

    def finish_in(f, cells, conv):
        gain = wide(gains[0], 2 * COLS)
        lanes = [slice(at * COLS, (at + 1) * COLS) for at in cells]
        image = jnp.concatenate([xs[f, :, at] for at in lanes], axis=1)
        grad = norm_pull(norm_parts(image, gain), gain, conv)
        for n, at in enumerate(cells):
            value = grad[:, n * COLS : (n + 1) * COLS] + dout[f, :, lanes[n]]
            gi_ref[f, pl.ds(at, C, stride=4), :] = value

    def backward_middle(f):
        finish_in(f, (1, 2), columns(dot(wt[...], middle_of(dob, f)), earlier, later))

    def backward_edges(f):
        window = edges_of(dob, dob_t, dob_b, f)
        finish_in(f, (0, 3), columns(dot(wt[...], window), earlier, later))

    on_core(start_scatter)

    for f in range(0, FR):
        backward_middle(f)

    on_core(start_z)

    whole(dob_t.at[pl.ds(0, FR)], ds.at[1], dr.at[0]).wait_recv()
    whole(dob_b.at[pl.ds(0, FR)], ds.at[0], dr.at[1]).wait_recv()

    @pl.when(me == 0)
    def _():
        dob_t[0:FR] = jnp.zeros((FR, C, COLS), BF16)

    @pl.when(me == slabs - 1)
    def _():
        dob_b[0:FR] = jnp.zeros((FR, C, COLS), BF16)

    for f in range(0, FR):
        backward_edges(f)

    on_core(gather)
    sums0_ref[...] = full[0][...]
    sums1_ref[...] = full[1][...]

    for side in range(2):
        pg_copy(side).wait_send()
        whole(hin_t, hs.at[side], hr.at[side, 0]).wait_send()
        whole(dob_t.at[pl.ds(0, FR)], ds.at[side], dr.at[side]).wait_send()
    on_core(sums_left)


def finish(slabs, gi_ref, sums0, sums1, out_hbm, gm_hbm, gh_hbm, grads, gm, gh, outs):
    gi_out = pltpu.make_async_copy(gi_ref, out_hbm, outs.at[3])
    gi_out.start()
    planes = slabs // 4
    scale = (1.0 / (FR * slabs * 4 * COLS)) ** 0.5
    for c, sums in enumerate((sums0, sums1)):
        for tile in tiles_of(c):
            if tile < 126:
                owner, rows = where_is(planes, tile)
                row, lane = divmod(tile, 7)
                value = sums[owner, rows].astype(F32) * scale
                grads[row * 16 : (row + 1) * 16, lane * COLS : (lane + 1) * COLS] = value
    gm_out = []
    for t in range(3):
        for y in range(3):
            for x in range(3):
                at = (y * 3 + t) * C
                gm[t, y, x] = grads[x * C : (x + 1) * C, at : at + C]
        gm_out.append(pltpu.make_async_copy(gm.at[t], gm_hbm.at[t], outs.at[t]))
        gm_out[t].start()
    head = jnp.concatenate([grads[n * C : (n + 1) * C, K3 : K3 + 32] for n in range(3)], axis=1)
    for y in range(3):
        for x in range(3):
            for t in range(3):
                at = y * 32 + x * 9 + t * 3
                gh[2 - t, y, x] = head[at : at + 3, :]
    gh_out = pltpu.make_async_copy(gh, gh_hbm, outs.at[4])
    gh_out.start()
    for copy in [gi_out, gh_out] + gm_out:
        copy.wait()


def local(slabs, *operands):
    (x, mc, hc, gin, gout, mw, hw, ag, tab, idx, order) = operands
    planes = slabs // 4
    share = [(planes, 16 * len(tiles_of(c)) // planes, COLS) for c in range(2)]
    hbm = pl.BlockSpec(memory_space=pltpu.HBM)
    vmem = pl.BlockSpec(memory_space=pltpu.VMEM)
    dma = pltpu.SemaphoreType.DMA
    operands = (
        x.reshape(FR, 4 * C, COLS),
        mc.reshape(2, 4 * C, COLS),
        hc.reshape(2, 4 * C, COLS),
        gin.reshape(1, C),
        gout.reshape(1, C),
        mw,
        hw,
        ag,
        jnp.transpose(tab, (1, 2, 0)),
        idx,
        order,
    )
    gi_shape = jax.ShapeDtypeStruct((FR, 4 * C, COLS), F32)
    gi, sums0, sums1 = pl.pallas_call(
        functools.partial(kernel, slabs),
        out_shape=(pltpu.VMEM(gi_shape.shape, F32),) + tuple(
            pltpu.VMEM(plane, BF16) for plane in share
        ),
        in_specs=[hbm] * 11,
        out_specs=[vmem] * 3,
        scratch_shapes=[pltpu.VMEM(value.shape, value.dtype) for value in operands[:8]]
        + [pltpu.SMEM(value.shape, value.dtype) for value in operands[8:]]
        + [
            pltpu.VMEM((FR, 4 * C, COLS), F32),
            pltpu.VMEM((FR, C, 4 * COLS), F32),
            pltpu.VMEM((2, C, COLS), F32),
            pltpu.VMEM((8, C, 4 * COLS), BF16),
            pltpu.VMEM((8, C, COLS), BF16),
            pltpu.VMEM((8, C, COLS), BF16),
            pltpu.VMEM((8, C, 4 * COLS), BF16),
            pltpu.VMEM((2, 3 * C, 7 * COLS), F32),
            pltpu.VMEM((3 * C, K3), BF16),
            pltpu.VMEM((3 * C, K3), BF16),
            pltpu.VMEM((C, C), BF16),
            pltpu.VMEM((4, 32, COLS), F32),
            pltpu.VMEM((4, 32, COLS), BF16),
            pltpu.VMEM((2, 32, COLS), BF16),
            pltpu.VMEM((8, 32, 6 * COLS), BF16),
            pltpu.VMEM((FR, C, 4 * COLS), F32),
            pltpu.VMEM((8, C, 4 * COLS), BF16),
            pltpu.VMEM((8, C, COLS), BF16),
            pltpu.VMEM((8, C, COLS), BF16),
            pltpu.VMEM((2, FR, 3 * C // 2, 2 * COLS), BF16),
            pltpu.VMEM((2, FR, 3 * C // 2, 2 * COLS), BF16),
            pltpu.VMEM((2, 3 * C // 2, K3), F32),
            pltpu.VMEM((C, C), F32),
            pltpu.VMEM((3 * C, 7 * COLS), F32),
            *[pltpu.VMEM(plane, BF16) for _ in range(4) for plane in share],
            *[pltpu.VMEM(plane[1:], BF16) for _ in range(2) for plane in share],
            *[pltpu.VMEM(plane, BF16) for plane in share],
            dma((11,)),
            dma((2,)),
            dma((2, 3)),
            dma((2,)),
            dma((2,)),
            dma((2,)),
            dma((2,)),
            dma,
            dma,
            dma((2,)),
            dma((2,)),
            dma((2,)),
            dma((2,)),
            dma((2,)),
            dma((2, (planes + 3) // 4)),
            dma,
            dma,
        ],
        compiler_params=pltpu.CompilerParams(
            collective_id=0, has_side_effects=True, vmem_limit_bytes=56 * 2**20
        ),
    )(*operands)
    gi, gm, gh = pl.pallas_call(
        functools.partial(finish, slabs),
        out_shape=(
            gi_shape,
            jax.ShapeDtypeStruct((3, 3, 3, C, C), F32),
            jax.ShapeDtypeStruct((3, 3, 3, 3, C), F32),
        ),
        in_specs=[vmem] * 3,
        out_specs=[hbm, hbm, hbm],
        scratch_shapes=[
            pltpu.VMEM((3 * C, 7 * COLS), F32),
            pltpu.VMEM((3, 3, 3, C, C), F32),
            pltpu.VMEM((3, 3, 3, 3, C), F32),
            dma((5,)),
        ],
        compiler_params=pltpu.CompilerParams(vmem_limit_bytes=16 * 2**20),
    )(gi, sums0, sums1)
    return gi.reshape(FR, C, 4, COLS), gm, gh


def solution(mesh):
    tile = P("video", None, "slab", None)
    whole = P("video", None, None, None, None)
    placed = (tile, tile, tile, P(), P(), P(), P(), tile, P(), P("video"), P())
    return jax.shard_map(
        functools.partial(local, mesh.shape["slab"]),
        mesh=mesh,
        in_specs=placed,
        out_specs=(tile, whole, whole),
        check_vma=False,
    )
```

```python
import functools

import jax
import jax.numpy as jnp
from jax import lax
from jax.experimental import pallas as pl
from jax.experimental.pallas import tpu as pltpu
from jax.sharding import PartitionSpec as P

EPS = 1e-06
MESH = pl.DeviceIdType.MESH
F32 = jnp.float32
BF16 = jnp.bfloat16
C = 96
FR = 6
COLS = 128
K3 = 9 * C


def dot(a, b):
    return lax.dot_general(a, b, (((1,), (0,)), ((), ())), preferred_element_type=F32)


def dot_nt(a, b):
    return lax.dot_general(a, b, (((1,), (1,)), ((), ())), preferred_element_type=F32)


def lane_of(value):
    return lax.broadcasted_iota(jnp.int32, value.shape, 1)


def later(value):
    return jnp.where(lane_of(value) == 0, 0.0, pltpu.roll(value, 1, 1))


def earlier(value):
    return jnp.where(lane_of(value) == COLS - 1, 0.0, pltpu.roll(value, COLS - 1, 1))


def by_row(shift, value):
    parts = [shift(value[:, i : i + COLS]) for i in range(0, value.shape[1], COLS)]
    return jnp.concatenate(parts, axis=1)


def wide(gain, width):
    return jnp.concatenate([gain] * (width // COLS), axis=1)


def norm_parts(value, gain):
    meansq = jnp.sum(value * value, axis=0, keepdims=True) * (1.0 / C)
    root = lax.rsqrt(meansq + EPS)
    unit = value * root
    normed = unit * gain
    sig = 0.5 * jnp.tanh(0.5 * normed) + 0.5
    return root, unit, normed, sig


def norm_pull(parts, gain, cot):
    root, unit, normed, sig = parts
    inner = cot * gain * (sig * (1.0 + normed * (1.0 - sig)))
    mean = jnp.sum(inner * unit, axis=0, keepdims=True) * (1.0 / C)
    return root * (inner - unit * mean)


def tiles_of(core):
    return range(0, 16) if core == 0 else range(16, 128)


def where_is(planes, tile):
    core = 0 if tile < 16 else 1
    tiles = tiles_of(core)
    owner, k = divmod(tile - tiles[0], len(tiles) // planes)
    return owner, slice(k * 16, (k + 1) * 16)


def kernel(
    slabs,
    x_hbm,
    mc_hbm,
    hc_hbm,
    gin_hbm,
    gout_hbm,
    mw_hbm,
    hw_hbm,
    ag_hbm,
    tab_hbm,
    idx_hbm,
    ord_hbm,
    gi_ref,
    sums0_ref,
    sums1_ref,
    x_ref,
    mc_ref,
    hc_ref,
    gin_ref,
    gout_ref,
    mw_ref,
    hw_ref,
    ag_ref,
    tab_ref,
    idx_ref,
    ord_ref,
    stage,
    xs,
    gains,
    hin,
    hin_t,
    hin_b,
    head,
    wtmp,
    wf,
    wt,
    hwt,
    pg_own,
    pg_send,
    pg_halo,
    taps,
    dout,
    dob,
    dob_t,
    dob_b,
    dsh_mid,
    dsh_edge,
    mid_grads,
    head_mid,
    grads,
    piece0,
    piece1,
    got10,
    got11,
    sum10,
    sum11,
    got20,
    got21,
    half30,
    half31,
    got30,
    got31,
    full0,
    full1,
    ins,
    hs,
    hr,
    ps,
    pr,
    ds,
    dr,
    s1,
    r1,
    s2,
    r2,
    s3,
    r3,
    s4,
    r4,
    s5,
    r5,
):
    me = lax.axis_index("slab")
    core = me % 2
    place = me % 4
    zh = place // 2
    xy = me // 4
    piece = (piece0, piece1)
    got1 = (got10, got11)
    sum1 = (sum10, sum11)
    got2 = (got20, got21)
    half3 = (half30, half31)
    got3 = (got30, got31)
    full = (full0, full1)
    planes = slabs // 4
    up = (me + slabs - 1) % slabs
    down = (me + 1) % slabs
    sibling = me + 1 - 2 * core
    zpartner = me + 2 - 4 * zh

    side_len = int(planes**0.5)
    px, py = xy % side_len, xy // side_len
    offsets = [(a, b) for a in range(side_len) for b in range(side_len)]
    offsets.sort(key=lambda at: -sum(min(step, side_len - step) for step in at))
    offsets = offsets[-1:] + offsets[:-1]

    def chip_at(k):
        a, b = offsets[k]
        return (py + a) % side_len * side_len + (px + b) % side_len

    def chip_from(k):
        a, b = offsets[k]
        return (py + side_len - a) % side_len * side_len + (px + side_len - b) % side_len

    def in_plane(k):
        return chip_at(k) * 4 + place

    pairs = (
        (x_hbm, x_ref),
        (mc_hbm, mc_ref),
        (hc_hbm, hc_ref),
        (gin_hbm, gin_ref),
        (gout_hbm, gout_ref),
        (mw_hbm, mw_ref),
        (hw_hbm, hw_ref),
        (ag_hbm, ag_ref),
        (tab_hbm, tab_ref),
        (idx_hbm, idx_ref),
        (ord_hbm, ord_ref),
    )
    loads = [pltpu.make_async_copy(a, b, ins.at[n]) for n, (a, b) in enumerate(pairs)]

    def remote(src, dst, send, recv, to):
        return pltpu.make_async_remote_copy(
            src_ref=src,
            dst_ref=dst,
            send_sem=send,
            recv_sem=recv,
            device_id={"slab": to},
            device_id_type=MESH,
        )

    barrier = pltpu.get_barrier_semaphore()

    def greet(to):
        pl.semaphore_signal(barrier, inc=1, device_id={"slab": to}, device_id_type=MESH)

    loads[1].start()
    greet(up)
    greet(down)
    greet(zpartner)
    for k in range(1, planes):
        greet(in_plane(k))
    for n in (0, 3, 8, 9, 10, 7, 2, 5, 6, 4):
        loads[n].start()

    def split_rows(f, source):
        stage[f] = source.astype(F32)
        return jnp.concatenate(
            [stage[f, pl.ds(r, C, stride=4), :] for r in range(4)], axis=1
        )

    loads[1].wait()
    for j in range(2):
        hin[j] = split_rows(j, mc_ref[j]).astype(BF16)

    def pg_copy(side):
        return remote(
            pg_send.at[0 if side == 0 else 3],
            pg_halo.at[1 - side],
            ps.at[side],
            pr.at[1 - side],
            up if side == 0 else down,
        )

    groups = (slice(0, 4), slice(4, 6), slice(6, 8))

    def hin_copy(side, f):
        group = 0 if f < 4 else 1 if f < 6 else 2
        if side == 0:
            row, there = hin.at[f, :, pl.ds(0, COLS)], hin_b.at[f]
            return remote(row, there, hs.at[0], hr.at[1, group], up)
        row, there = hin.at[f, :, pl.ds(3 * COLS, COLS)], hin_t.at[f]
        return remote(row, there, hs.at[1], hr.at[0, group], down)

    def whole(ref, send, recv):
        return remote(ref, ref, send, recv, sibling)

    def dob_copy(side, f):
        if side == 0:
            row, there = dob.at[f, :, pl.ds(0, COLS)], dob_b.at[f]
            return remote(row, there, ds.at[0], dr.at[1], up)
        row, there = dob.at[f, :, pl.ds(3 * COLS, COLS)], dob_t.at[f]
        return remote(row, there, ds.at[1], dr.at[0], down)

    pl.semaphore_wait(barrier, planes + 2)
    def halo(far, frames):
        for c in range(2):

            @pl.when(core == c)
            def _():
                for f in frames:
                    hin_copy(c if far else 1 - c, f).start()

    halo(True, range(2))

    for n in (7, 8, 9, 10):
        loads[n].wait()
    pg_own[...] = jnp.zeros_like(pg_own)
    for f in range(FR):
        picked = []
        for a in range(4):
            total = None
            for j in range(FR):
                weight = jnp.where(ord_ref[j] == f, 1.0, 0.0).astype(F32)
                term = ag_ref[j, a].astype(F32) * weight
                total = term if total is None else total + term
            picked.append(total)
        row = idx_ref[f]
        for c in range(3):
            value = picked[0] * tab_ref[c, 0, row]
            for a in range(1, 4):
                value = value + picked[a] * tab_ref[c, a, row]
            for r in range(4):
                pg_own[r, 6 + 3 * f + c : 7 + 3 * f + c, :] = value[r : r + 1, :]
    pg_send[...] = pg_own[...].astype(BF16)
    loads[0].wait()
    loads[3].wait()
    gains[0] = jnp.broadcast_to(gin_ref[...], (COLS, C)).T
    for side in range(2):
        pg_copy(side).start()

    def make_h(f):
        value = split_rows(f, x_ref[f])
        xs[f] = value
        _, _, normed, sig = norm_parts(value, wide(gains[0], 4 * COLS))
        hin[f + 2] = (normed * sig).astype(BF16)

    for f in range(0, FR):
        make_h(f)
        if f % 2 == 1:
            halo(True, range(f + 1, f + 3))
    halo(False, range(8))

    loads[4].wait()
    gains[1] = jnp.broadcast_to(gout_ref[...], (COLS, C)).T

    loads[5].wait()
    for x in range(3):
        for y in range(3):
            for t in range(3):
                at = (y * 3 + t) * C
                wtmp[0, x * C : (x + 1) * C, at : at + C] = mw_ref[t, y, x].astype(F32)
                wtmp[1, x * C : (x + 1) * C, at : at + C] = mw_ref[2 - t, 2 - y, x].astype(F32).T
    wf[...] = wtmp[0, :, 0:K3].astype(BF16)
    wt[...] = wtmp[1, :, 0:K3].astype(BF16)
    loads[6].wait()
    grads[0:C, 0:C] = jnp.zeros((C, C), F32)
    for y in range(3):
        for x in range(3):
            for t in range(3):
                at = y * 32 + x * 9 + t * 3
                grads[at : at + 3, 0:C] = hw_ref[2 - t, y, x].astype(F32)
    hwt[...] = grads[0:C, 0:C].T.astype(BF16)
    loads[2].wait()
    for j in range(2):
        head[j] = split_rows(j, hc_ref[j]).astype(BF16)

    out_row = lax.broadcasted_iota(jnp.int32, (8 * 32, C), 0)
    in_row = lax.broadcasted_iota(jnp.int32, (8 * 32, C), 1)
    frame = lax.shift_right_logical(out_row, 5)
    tap = out_row - 32 * frame
    col = jnp.where(tap >= 9, 1, 0) + jnp.where(tap >= 18, 1, 0)
    source = col * 32 + frame * 3 + (tap - 9 * col)
    chosen = jnp.where((in_row == source) & (tap < 27), 1.0, 0.0).astype(BF16)

    def spread(rows, lanes):
        rows = [value.astype(F32) for value in rows]
        stack = jnp.concatenate(
            [
                jnp.concatenate([earlier(value) for value in rows], axis=1),
                jnp.concatenate(rows, axis=1),
                jnp.concatenate([later(value) for value in rows], axis=1),
            ],
            axis=0,
        )
        result = dot(chosen, stack.astype(BF16)).astype(BF16)
        for f in range(8):
            for n, at in enumerate(lanes):
                value = result[f * 32 : (f + 1) * 32, n * COLS : (n + 1) * COLS]
                taps[f, :, at * COLS : (at + 1) * COLS] = value

    spread([pg_send[r] for r in range(4)], (1, 2, 3, 4))

    def pixel_taps(f, first, rows):
        return jnp.concatenate(
            [taps[f, :, pl.ds((2 - y + first) * COLS, rows * COLS)] for y in range(3)], axis=0
        )

    def finish_out(f, cells, image, conv, cot, shifted):
        gain = wide(gains[1], 2 * COLS)
        out = image + conv
        parts = norm_parts(out, gain)
        hh = (parts[2] * parts[3]).astype(BF16)
        grad = norm_pull(parts, gain, cot)
        before = by_row(earlier, grad).astype(BF16)
        after = by_row(later, grad).astype(BF16)
        here = grad.astype(BF16)
        for n, at in enumerate(cells):
            part = slice(n * COLS, (n + 1) * COLS)
            lanes = slice(at * COLS, (at + 1) * COLS)
            head[f + 2, :, lanes] = hh[:, part]
            dout[f, :, lanes] = grad[:, part]
            dob[f, :, lanes] = here[:, part]
        shifted[0, f, 0:C] = before
        shifted[0, f, C : 3 * C // 2] = here[0 : C // 2]
        shifted[1, f, 0 : C // 2] = here[C // 2 : C]
        shifted[1, f, C // 2 : 3 * C // 2] = after

    def columns(z, first, last):
        return z[C : 2 * C] + by_row(first, z[0:C]) + by_row(last, z[2 * C : 3 * C])

    def middle_of(field, f):
        return jnp.concatenate(
            [field[f + t, :, y * COLS : (y + 2) * COLS] for y in range(3) for t in range(3)], axis=0
        )

    def edges_of(field, top, bottom, f):
        parts = []
        for y in range(3):
            for t in range(3):
                one = top[f + t] if y == 0 else field[f + t, :, (y - 1) * COLS : y * COLS]
                two = bottom[f + t] if y == 2 else field[f + t, :, (y + 2) * COLS : (y + 3) * COLS]
                parts.append(jnp.concatenate([one, two], axis=1))
        return jnp.concatenate(parts, axis=0)

    def forward_middle(f):
        conv = columns(dot(wf[...], middle_of(hin, f)), later, earlier)
        cot = dot(hwt[...], pixel_taps(f + 2, 1, 2))
        finish_out(f, (1, 2), xs[f, :, COLS : 3 * COLS], conv, cot, dsh_mid)

    for f in range(0, FR):
        forward_middle(f)

    def edge_windows(frames):
        return jnp.concatenate([edges_of(hin, hin_t, hin_b, f) for f in frames], axis=1)

    def edge_grads(half, frames):
        return jnp.concatenate([dsh_edge[half, f] for f in frames], axis=1)

    shifted = [
        jnp.concatenate([dsh_mid[half, f] for f in range(FR)], axis=1) for half in range(2)
    ]
    middle = dot_nt(
        jnp.concatenate(shifted, axis=0),
        jnp.concatenate([middle_of(hin, f) for f in range(FR)], axis=1),
    )
    mid_grads[0] = middle[0 : 3 * C // 2]
    mid_grads[1] = middle[3 * C // 2 : 3 * C]

    def head_edge_taps(f):
        return jnp.concatenate([pixel_taps(f, 0, 1), pixel_taps(f, 3, 1)], axis=1)

    def head_edges(f):
        return jnp.concatenate([head[f, :, 0:COLS], head[f, :, 3 * COLS : 4 * COLS]], axis=1)

    head_mid[...] = dot_nt(
        jnp.concatenate([pixel_taps(f, 1, 2) for f in range(8)], axis=1),
        jnp.concatenate([head[f, :, COLS : 3 * COLS] for f in range(8)], axis=1),
    )

    def hin_arrived(group):
        some = groups[group]
        shape = (some.stop - some.start, C, COLS)
        span = pl.ds(some.start, shape[0])
        whole(hin_t.at[span], hs.at[1], hr.at[0, group]).wait_recv()
        whole(hin_b.at[span], hs.at[0], hr.at[1, group]).wait_recv()

        @pl.when(me == 0)
        def _():
            hin_t[some] = jnp.zeros(shape, BF16)

        @pl.when(me == slabs - 1)
        def _():
            hin_b[some] = jnp.zeros(shape, BF16)

    for side in range(2):
        pg_copy(side).wait_recv()

    @pl.when(me == 0)
    def _():
        pg_halo[0] = jnp.zeros((32, COLS), BF16)

    @pl.when(me == slabs - 1)
    def _():
        pg_halo[1] = jnp.zeros((32, COLS), BF16)

    spread([pg_halo[0], pg_halo[1]], (0, 5))

    def forward_edges(f):
        conv = columns(dot(wf[...], edges_of(hin, hin_t, hin_b, f)), later, earlier)
        cot = dot(hwt[...], head_edge_taps(f + 2))
        image = jnp.concatenate([xs[f, :, 0:COLS], xs[f, :, 3 * COLS : 4 * COLS]], axis=1)
        finish_out(f, (0, 3), image, conv, cot, dsh_edge)

    def head_part(frames):
        return dot_nt(
            jnp.concatenate([head_edge_taps(f) for f in frames], axis=1),
            jnp.concatenate([head_edges(f) for f in frames], axis=1),
        )

    late = range(4, FR)
    for group in range(3):
        frames = range(2 * group, 2 * group + 2)
        hin_arrived(group)
        for f in frames:
            forward_edges(f)
        for f in frames:
            for side in range(2):
                dob_copy(side, f).start()
        if group < 2:
            part = dot_nt(
                jnp.concatenate([edge_grads(0, frames), edge_grads(1, frames)], axis=0),
                edge_windows(frames),
            )
            mid_grads[0] += part[0 : 3 * C // 2]
            mid_grads[1] += part[3 * C // 2 : 3 * C]
        if group == 1:
            head_mid[...] += head_part(range(6))

    total = head_mid[...] + head_part(range(6, 8))
    part = dot_nt(
        jnp.concatenate([edge_grads(0, late), edge_grads(1, late)], axis=0), edge_windows(late)
    )
    for half in range(2):
        rows = slice(half * (3 * C // 2), (half + 1) * (3 * C // 2))
        grads[rows, 0:K3] = mid_grads[half] + part[rows]
    for n in range(3):
        grads[n * C : (n + 1) * C, K3 : K3 + 32] = total[:, n * 32 : (n + 1) * 32]

    def tile_of(tile):
        row, lane = divmod(tile, 7)
        return grads[row * 16 : (row + 1) * 16, lane * COLS : (lane + 1) * COLS]

    def pair_copy(c):
        return remote(piece[1 - c], got1[1 - c], s1, r1, sibling)

    def parts_of(c):
        rows = 16 * len(tiles_of(c)) // planes
        cut = (rows // 16 + 1) // 2 * 16
        return [span for span in (pl.ds(0, cut), pl.ds(cut, rows - cut)) if span.size]

    def scatter_copy(c, k, n):
        span = parts_of(c)[n]
        there = got2[c].at[k, span]
        return remote(sum1[c].at[chip_at(k), span], there, s2.at[n], r2.at[n], in_plane(k))

    def z_copy(c, n):
        span = parts_of(c)[n]
        return remote(half3[c].at[span], got3[c].at[span], s3.at[n], r3.at[n], zpartner)

    def gather_copy(c, k, n):
        mine = full[c].at[xy, parts_of(c)[n]]
        return remote(mine, mine, s4.at[n], r4.at[n, k // 4], in_plane(k))

    def pass_on(c, k, n):
        one = full[c].at[chip_from(k), parts_of(c)[n]]
        return remote(one, one, s5, r5, sibling)

    def others(c, n, low=1, high=planes):
        return got2[c].at[pl.ds(low, high - low), parts_of(c)[n]]

    def on_core(stage):
        for c in range(2):
            pl.when(core == c)(functools.partial(stage, c))

    def start_pair(c):
        for tile in tiles_of(1 - c):
            owner, rows = where_is(planes, tile)
            value = tile_of(tile).astype(BF16) if tile < 126 else jnp.zeros((16, COLS), BF16)
            piece[1 - c][owner, rows] = value
        pair_copy(c).start()

    def start_scatter(c):
        whole(got1[c], s1, r1).wait_recv()
        for tile in tiles_of(c):
            owner, rows = where_is(planes, tile)
            value = got1[c][owner, rows].astype(F32)
            if tile < 126:
                value = value + tile_of(tile)
            sum1[c][owner, rows] = value.astype(BF16)
        for n in range(len(parts_of(c))):
            for k in range(1, planes):
                scatter_copy(c, k, n).start()

    def start_z(c):
        for n, span in enumerate(parts_of(c)):
            whole(others(c, n), s2.at[n], r2.at[n]).wait_recv()
            total = sum1[c][xy, span].astype(F32)
            for k in range(1, planes):
                total = total + got2[c][k, span].astype(F32)
            half3[c][span] = total.astype(BF16)
            z_copy(c, n).start()

    def gather(c):
        for n, span in enumerate(parts_of(c)):
            z_copy(c, n).wait_recv()
            both = half3[c][span].astype(F32) + got3[c][span].astype(F32)
            full[c][xy, span] = both.astype(BF16)
            for k in range(1, planes):
                gather_copy(c, k, n).start()
            pass_on(c, 0, n).start()
        for n in range(len(parts_of(c))):
            for low in range(0, planes, 4):
                some = range(max(low, 1), min(low + 4, planes))
                arrived = others(c, n, 0, len(some))
                whole(arrived, s4.at[n], r4.at[n, low // 4]).wait_recv()
                for k in some:
                    pass_on(c, k, n).start()
        whole(full[1 - c], s5, r5).wait_recv()

    def sums_left(c):
        pair_copy(c).wait_send()
        for n in range(len(parts_of(c))):
            whole(others(c, n), s2.at[n], r2.at[n]).wait_send()
            z_copy(c, n).wait_send()
            whole(others(c, n), s4.at[n], r4.at[n, 0]).wait_send()
        whole(full[c], s5, r5).wait_send()

    on_core(start_pair)

    dob[6] = jnp.zeros((C, 4 * COLS), BF16)
    dob[7] = jnp.zeros((C, 4 * COLS), BF16)
    for f in (6, 7):
        dob_t[f] = jnp.zeros((C, COLS), BF16)
        dob_b[f] = jnp.zeros((C, COLS), BF16)

    def finish_in(f, cells, conv):
        gain = wide(gains[0], 2 * COLS)
        lanes = [slice(at * COLS, (at + 1) * COLS) for at in cells]
        image = jnp.concatenate([xs[f, :, at] for at in lanes], axis=1)
        grad = norm_pull(norm_parts(image, gain), gain, conv)
        for n, at in enumerate(cells):
            value = grad[:, n * COLS : (n + 1) * COLS] + dout[f, :, lanes[n]]
            gi_ref[f, pl.ds(at, C, stride=4), :] = value

    def backward_middle(f):
        finish_in(f, (1, 2), columns(dot(wt[...], middle_of(dob, f)), earlier, later))

    def backward_edges(f):
        window = edges_of(dob, dob_t, dob_b, f)
        finish_in(f, (0, 3), columns(dot(wt[...], window), earlier, later))

    on_core(start_scatter)

    for f in range(0, FR):
        backward_middle(f)

    on_core(start_z)

    whole(dob_t.at[pl.ds(0, FR)], ds.at[1], dr.at[0]).wait_recv()
    whole(dob_b.at[pl.ds(0, FR)], ds.at[0], dr.at[1]).wait_recv()

    @pl.when(me == 0)
    def _():
        dob_t[0:FR] = jnp.zeros((FR, C, COLS), BF16)

    @pl.when(me == slabs - 1)
    def _():
        dob_b[0:FR] = jnp.zeros((FR, C, COLS), BF16)

    for f in range(0, FR):
        backward_edges(f)

    on_core(gather)
    sums0_ref[...] = full[0][...]
    sums1_ref[...] = full[1][...]

    for side in range(2):
        pg_copy(side).wait_send()
        whole(hin_t, hs.at[side], hr.at[side, 0]).wait_send()
        whole(dob_t.at[pl.ds(0, FR)], ds.at[side], dr.at[side]).wait_send()
    on_core(sums_left)


def finish(slabs, gi_ref, sums0, sums1, out_hbm, gm_hbm, gh_hbm, grads, gm, gh, outs):
    gi_out = pltpu.make_async_copy(gi_ref, out_hbm, outs.at[0])
    for f in range(FR):
        pltpu.make_async_copy(gi_ref.at[f], out_hbm.at[f], outs.at[0]).start()
    planes = slabs // 4
    scale = (1.0 / (FR * slabs * 4 * COLS)) ** 0.5
    for c, sums in enumerate((sums0, sums1)):
        for tile in tiles_of(c):
            if tile < 126:
                owner, rows = where_is(planes, tile)
                row, lane = divmod(tile, 7)
                value = sums[owner, rows].astype(F32) * scale
                grads[row * 16 : (row + 1) * 16, lane * COLS : (lane + 1) * COLS] = value
    gm_out = pltpu.make_async_copy(gm, gm_hbm, outs.at[1])
    for t in range(3):
        for y in range(3):
            for x in range(3):
                at = (y * 3 + t) * C
                gm[t, y, x] = grads[x * C : (x + 1) * C, at : at + C]
            pltpu.make_async_copy(gm.at[t, y], gm_hbm.at[t, y], outs.at[1]).start()
    head = jnp.concatenate([grads[n * C : (n + 1) * C, K3 : K3 + 32] for n in range(3)], axis=1)
    for y in range(3):
        for x in range(3):
            for t in range(3):
                at = y * 32 + x * 9 + t * 3
                gh[2 - t, y, x] = head[at : at + 3, :]
    gh_out = pltpu.make_async_copy(gh, gh_hbm, outs.at[2])
    gh_out.start()
    for copy in (gi_out, gm_out, gh_out):
        copy.wait()


def local(slabs, *operands):
    (x, mc, hc, gin, gout, mw, hw, ag, tab, idx, order) = operands
    planes = slabs // 4
    share = [(planes, 16 * len(tiles_of(c)) // planes, COLS) for c in range(2)]
    hbm = pl.BlockSpec(memory_space=pltpu.HBM)
    vmem = pl.BlockSpec(memory_space=pltpu.VMEM)
    dma = pltpu.SemaphoreType.DMA
    operands = (
        x.reshape(FR, 4 * C, COLS),
        mc.reshape(2, 4 * C, COLS),
        hc.reshape(2, 4 * C, COLS),
        gin.reshape(1, C),
        gout.reshape(1, C),
        mw,
        hw,
        ag,
        jnp.transpose(tab, (1, 2, 0)),
        idx,
        order,
    )
    gi_shape = jax.ShapeDtypeStruct((FR, 4 * C, COLS), F32)
    gi, sums0, sums1 = pl.pallas_call(
        functools.partial(kernel, slabs),
        out_shape=(pltpu.VMEM(gi_shape.shape, F32),) + tuple(
            pltpu.VMEM(plane, BF16) for plane in share
        ),
        in_specs=[hbm] * 11,
        out_specs=[vmem] * 3,
        scratch_shapes=[pltpu.VMEM(value.shape, value.dtype) for value in operands[:8]]
        + [pltpu.SMEM(value.shape, value.dtype) for value in operands[8:]]
        + [
            pltpu.VMEM((FR, 4 * C, COLS), F32),
            pltpu.VMEM((FR, C, 4 * COLS), F32),
            pltpu.VMEM((2, C, COLS), F32),
            pltpu.VMEM((8, C, 4 * COLS), BF16),
            pltpu.VMEM((8, C, COLS), BF16),
            pltpu.VMEM((8, C, COLS), BF16),
            pltpu.VMEM((8, C, 4 * COLS), BF16),
            pltpu.VMEM((2, 3 * C, 7 * COLS), F32),
            pltpu.VMEM((3 * C, K3), BF16),
            pltpu.VMEM((3 * C, K3), BF16),
            pltpu.VMEM((C, C), BF16),
            pltpu.VMEM((4, 32, COLS), F32),
            pltpu.VMEM((4, 32, COLS), BF16),
            pltpu.VMEM((2, 32, COLS), BF16),
            pltpu.VMEM((8, 32, 6 * COLS), BF16),
            pltpu.VMEM((FR, C, 4 * COLS), F32),
            pltpu.VMEM((8, C, 4 * COLS), BF16),
            pltpu.VMEM((8, C, COLS), BF16),
            pltpu.VMEM((8, C, COLS), BF16),
            pltpu.VMEM((2, FR, 3 * C // 2, 2 * COLS), BF16),
            pltpu.VMEM((2, FR, 3 * C // 2, 2 * COLS), BF16),
            pltpu.VMEM((2, 3 * C // 2, K3), F32),
            pltpu.VMEM((C, C), F32),
            pltpu.VMEM((3 * C, 7 * COLS), F32),
            *[pltpu.VMEM(plane, BF16) for _ in range(4) for plane in share],
            *[pltpu.VMEM(plane[1:], BF16) for _ in range(2) for plane in share],
            *[pltpu.VMEM(plane, BF16) for plane in share],
            dma((11,)),
            dma((2,)),
            dma((2, 3)),
            dma((2,)),
            dma((2,)),
            dma((2,)),
            dma((2,)),
            dma,
            dma,
            dma((2,)),
            dma((2,)),
            dma((2,)),
            dma((2,)),
            dma((2,)),
            dma((2, (planes + 3) // 4)),
            dma,
            dma,
        ],
        compiler_params=pltpu.CompilerParams(
            collective_id=0, has_side_effects=True, vmem_limit_bytes=56 * 2**20
        ),
    )(*operands)
    gi, gm, gh = pl.pallas_call(
        functools.partial(finish, slabs),
        out_shape=(
            gi_shape,
            jax.ShapeDtypeStruct((3, 3, 3, C, C), F32),
            jax.ShapeDtypeStruct((3, 3, 3, 3, C), F32),
        ),
        in_specs=[vmem] * 3,
        out_specs=[hbm, hbm, hbm],
        scratch_shapes=[
            pltpu.VMEM((3 * C, 7 * COLS), F32),
            pltpu.VMEM((3, 3, 3, C, C), F32),
            pltpu.VMEM((3, 3, 3, 3, C), F32),
            dma((3,)),
        ],
        compiler_params=pltpu.CompilerParams(vmem_limit_bytes=16 * 2**20),
    )(gi, sums0, sums1)
    return gi.reshape(FR, C, 4, COLS), gm, gh


def solution(mesh):
    tile = P("video", None, "slab", None)
    whole = P("video", None, None, None, None)
    placed = (tile, tile, tile, P(), P(), P(), P(), tile, P(), P("video"), P())
    return jax.shard_map(
        functools.partial(local, mesh.shape["slab"]),
        mesh=mesh,
        in_specs=placed,
        out_specs=(tile, whole, whole),
        check_vma=False,
    )
```
